128 devices in a mesh: ao: 8 (over y, core), aux: 16 (over z, x).
Axes of the slice: x: 4, y: 4, z: 4, core: 2. Of those that a mesh axis runs over, the one named last changes fastest.
Arguments:
- three_centre: bfloat16 [32768, 4096], P('ao', 'aux'), may hold values from -1 to 1
- tile_list: int32 [8, 32], P('ao', 'aux'), may hold values 0 or 1
- pair_blocks: int32 [8, 2], P('ao'), may hold values from 0 to 15
- green_occ: bfloat16 [16, 64, 64], replicated, may hold values from -0.75 to 0.75
- green_virt: bfloat16 [16, 64, 64], replicated, may hold values from -0.75 to 0.75
Outputs:
- polarizability: float32 [4096, 4096], P('aux', 'ao')
The draws below stay inside these ranges and needn't reach their ends.
All inputs are finite; a program needn't handle non-finite values. No bound on the sum of `tile_list` on one device may be relied on, other than what follows from the above.
Results may differ from the reference program's by a relative error of at most 0.0041.
Values may be sent and summed in bfloat16 or wider, within the bound.
No kernel may reach another device: no remote copies, remote signals or barrier semaphores. Data moves between devices by JAX's collectives and lax.ppermute only.
A program may use at most 128 MiB of HBM per device.

```python
import jax
import jax.numpy as jnp
from jax import lax

BA = 64
BP = 128
NPAIR = 8
NBLK = 16
NAUX = 4096


def plant(values, rng, low, high):
    shape = values.shape
    place = [jax.random.randint(jax.random.fold_in(rng, axis), (), 0, shape[axis]) for axis in range(len(shape))]
    values = values.at[tuple(place)].set(low)
    longest = shape.index(max(shape))
    place[longest] = (place[longest] + 1) % shape[longest]
    return values.at[tuple(place)].set(high)


def shard_levels(own_key, dims, split, low, top_value):
    loudness = 1.0
    for position, blocks in split:
        draws = jax.random.uniform(jax.random.fold_in(jax.random.fold_in(own_key, 6), position), (blocks,), jnp.float32, low / len(split), top_value / len(split))
        loudness = loudness * jnp.repeat(jnp.exp(draws), dims[position] // blocks).reshape((-1,) + (1,) * (len(dims) - 1 - position))
    return loudness


def scatter_about(key, dims, scale, most, pieces=(), dtype=jnp.bfloat16):
    level = shard_levels(key, dims, pieces, -0.22, 0.18) if pieces else 1.0
    drawn = jax.random.normal(key, dims, jnp.float32) * scale * level
    return jnp.minimum(jnp.maximum(drawn, -most), most).astype(dtype)


def setup_inputs(seed: int = 0) -> dict:
    arg_keys = jax.random.split(jax.random.key(seed), 6)
    three_centre = scatter_about(arg_keys[0], (NPAIR * BA * BA, NAUX), ((NPAIR * BA * BA) ** -0.25), 1.0, ((0, 8), (1, 16)))
    tile_list = plant((jax.random.randint(arg_keys[1], (NPAIR, NAUX // BP), 0, 2) < 1).astype(jnp.int32), jax.random.fold_in(arg_keys[1], 1), 0, 1)
    pair_blocks = plant(jax.random.randint(arg_keys[2], (NPAIR, 2), 0, NBLK), jax.random.fold_in(arg_keys[2], 1), 0, NBLK - 1).astype(jnp.int32)
    green_occ = scatter_about(arg_keys[3], (NBLK, BA, BA), BA ** -0.5, 0.75)
    green_virt = scatter_about(arg_keys[4], (NBLK, BA, BA), BA ** -0.5, 0.75)
    return {"three_centre": three_centre, "tile_list": tile_list, "pair_blocks": pair_blocks, "green_occ": green_occ, "green_virt": green_virt}


def reference(three_centre, tile_list, pair_blocks, green_occ, green_virt):
    tiles = three_centre.reshape(NPAIR, BA, BA, NAUX // BP, BP)
    masked = tiles * tile_list.astype(jnp.bfloat16)[:, None, None, :, None]
    masked = masked.reshape(NPAIR, BA, BA, NAUX)
    occ_all = green_occ[pair_blocks[:, 0]]
    virt_all = green_virt[pair_blocks[:, 1]]

    def one_pair(total, items):
        block, occ, virt = items
        half = jnp.einsum('lm,mnc->lnc', occ.astype(jnp.float32), block.astype(jnp.float32)).astype(jnp.bfloat16)
        contracted = jnp.einsum('lnc,sn->lsc', half.astype(jnp.float32), virt.astype(jnp.float32)).astype(jnp.bfloat16)
        left = block.reshape(BA * BA, NAUX)
        right = contracted.reshape(BA * BA, NAUX)
        return total + jnp.dot(left.T, right, preferred_element_type=jnp.float32), None

    start = jnp.zeros((NAUX, NAUX), jnp.float32)
    total, unused = lax.scan(one_pair, start, (masked, occ_all, virt_all))
    return -2.0 * total
```

```python
import functools

import jax
import jax.numpy as jnp
from jax import lax
from jax.experimental import pallas as pl
from jax.experimental.pallas import tpu as pltpu
from jax.sharding import Mesh, PartitionSpec as P

SIDE = 4
BLOCK = 256


def pick_blocks(indices, table):
    blocks_total, width = (table.shape[0], table.shape[1])
    onehot = (indices[:, None] == jnp.arange(blocks_total)[None, :]).astype(jnp.bfloat16)
    picked = jnp.dot(
        onehot, table.reshape(blocks_total, width * width), preferred_element_type=jnp.float32
    )
    return picked.astype(jnp.bfloat16).reshape(indices.shape[0], width, width)


def contract(tiles, occ, virt):
    width = occ.shape[-1]
    cols = tiles.shape[1]
    half = jnp.dot(
        occ, tiles.reshape(width, width * cols), preferred_element_type=jnp.float32
    ).astype(jnp.bfloat16)
    return (
        jnp.einsum(
            "lnc,sn->lsc",
            half.reshape(width, width, cols),
            virt,
            preferred_element_type=jnp.float32,
        )
        .astype(jnp.bfloat16)
        .reshape(width * width, cols)
    )


def products_kernel(steps, where, *refs):
    a_refs, b_refs = refs[0:5], refs[5:10]
    keep_ref, send_ref, acc = refs[10:]
    k = pl.program_id(0)

    @pl.when(k == 0)
    def _():
        acc[...] = jnp.zeros_like(acc)

    def block(blocks, offset):
        if offset == 2:
            return jnp.where(k < steps // 2, blocks[3][...], blocks[4][...])
        return blocks[{0: 0, 1: 1, 3: 2}[offset]][...]

    rights = [block(b_refs, q) for q in range(SIDE)]
    for p in range(SIDE):
        left = block(a_refs, p).T
        for q in range(SIDE):
            acc[where[q], where[SIDE + p]] += jnp.dot(
                left, rights[q], preferred_element_type=jnp.float32
            )

    @pl.when(k == steps - 1)
    def _():
        keep_ref[...] = acc[0:2]
        send_ref[...] = acc[2:4].astype(jnp.bfloat16)


def products(where, lefts, rights):
    rows = lefts[0].shape[0]
    chunk = 512
    steps = rows // chunk
    whole = pl.BlockSpec((chunk, BLOCK), lambda k, where: (k, 0))
    first = pl.BlockSpec((chunk, BLOCK), lambda k, where: (jnp.minimum(k, steps // 2 - 1), 0))
    second = pl.BlockSpec((chunk, BLOCK), lambda k, where: (jnp.maximum(k - steps // 2, 0), 0))
    five = [whole, whole, whole, first, second]
    shape = (2, SIDE, BLOCK, BLOCK)
    out = pl.BlockSpec(shape, lambda k, where: (0, 0, 0, 0))
    return pl.pallas_call(
        functools.partial(products_kernel, steps),
        grid_spec=pltpu.PrefetchScalarGridSpec(
            num_scalar_prefetch=1,
            grid=(steps,),
            in_specs=five + five,
            out_specs=[out, out],
            scratch_shapes=[pltpu.VMEM((SIDE, SIDE, BLOCK, BLOCK), jnp.float32)],
        ),
        out_shape=[
            jax.ShapeDtypeStruct(shape, jnp.float32),
            jax.ShapeDtypeStruct(shape, jnp.bfloat16),
        ],
        compiler_params=pltpu.CompilerParams(vmem_limit_bytes=48 * 2**20),
        cost_estimate=pl.CostEstimate(
            flops=2 * rows * 1024 * 1024, bytes_accessed=20 * 2**20, transcendentals=0
        ),
    )(where, *lefts, *rights)


def around(block, axis):
    half = block.shape[0] // 2
    take_next = [((i + 1) % SIDE, i) for i in range(SIDE)]
    take_prev = [((i - 1) % SIDE, i) for i in range(SIDE)]
    after = lax.ppermute(block, axis, take_next)
    before = lax.ppermute(block, axis, take_prev)
    far_low = lax.ppermute(after[:half], axis, take_next)
    far_high = lax.ppermute(before[half:], axis, take_prev)
    return [block, after, before, far_low, far_high]


def per_device(three_centre, tile_list, pair_blocks, green_occ, green_virt):
    y, c, z, x = (lax.axis_index(name) for name in ("y", "c", "z", "x"))
    weights = jnp.repeat(tile_list[0].astype(jnp.bfloat16), BLOCK // tile_list.shape[1])
    tiles = three_centre * weights[None, :]
    occ = pick_blocks(pair_blocks[:, 0], green_occ)[0]
    virt = pick_blocks(pair_blocks[:, 1], green_virt)[0]
    lefts = around(tiles, "z")
    rights = around(contract(tiles, occ, virt), "x")

    column = (x + jnp.arange(SIDE)) & 3
    slot = jnp.where(column // 2 == c, 0, 2) + column % 2
    where = jnp.concatenate([slot, (z + jnp.arange(SIDE)) & 3]).astype(jnp.int32)
    keep, send = products(where, lefts, rights)

    total = keep + lax.ppermute(send, "c", [(0, 1), (1, 0)]).astype(jnp.float32)
    quarter = BLOCK // SIDE
    total = total.reshape(2, SIDE, SIDE, quarter, BLOCK)
    own = lax.dynamic_index_in_dim(total, y, 2, keepdims=False)
    for k in range(1, SIDE):
        piece = lax.dynamic_index_in_dim(total, (y + k) & 3, 2, keepdims=False)
        moved = lax.ppermute(
            piece.astype(jnp.bfloat16), "y", [(i, (i + k) % SIDE) for i in range(SIDE)]
        )
        own = own + moved.astype(jnp.float32)
    own = -2.0 * own

    arrived = []
    for k in range(SIDE):
        piece = lax.dynamic_index_in_dim(own, (y + k) & 3, 1, keepdims=False)
        perm = [
            (i * SIDE + j, j * SIDE + (i + k) % SIDE) for i in range(SIDE) for j in range(SIDE)
        ]
        arrived.append(lax.ppermute(piece, ("y", "z"), perm))
    stacked = jnp.stack(arrived[::-1] + arrived[:0:-1])
    ordered = lax.dynamic_slice_in_dim(stacked, (SIDE - 1 - z) & 3, SIDE, 0)
    return ordered.transpose(0, 2, 1, 3).reshape(BLOCK, 2 * BLOCK)


def solution(mesh):
    fine = Mesh(mesh.devices.reshape(SIDE, 2, SIDE, SIDE), ("y", "c", "z", "x"))
    ao, aux = ("y", "c"), ("z", "x")
    return jax.shard_map(
        per_device,
        mesh=fine,
        in_specs=(P(ao, aux), P(ao, aux), P(ao, None), P(), P()),
        out_specs=P(aux, ao),
        check_vma=False,
    )
```

```python
import functools

import jax
import jax.numpy as jnp
from jax import lax
from jax.experimental import pallas as pl
from jax.experimental.pallas import tpu as pltpu
from jax.sharding import Mesh, PartitionSpec as P

SIDE = 4
BLOCK = 256
HALF = BLOCK // 2
NEAR = (0, 1, 3)
LATE = tuple((2, q) for q in NEAR + (2,)) + tuple((p, 2) for p in NEAR)
F32 = jnp.float32
BF16 = jnp.bfloat16


def iota(shape, dim):
    return lax.broadcasted_iota(jnp.int32, shape, dim)


def contract_kernel(width, group, scalars, tiles_ref, occ_ref, virt_ref, out_ref, half_ref):
    cols = tiles_ref.shape[1]
    tall = width * group
    spread = jnp.where(iota((tall, width), 0) // group == iota((tall, width), 1), 1.0, 0.0).astype(BF16)
    rows = jnp.dot(spread, occ_ref[0], preferred_element_type=F32).astype(BF16)
    wide = lax.dot_general(
        rows, spread, (((1,), (1,)), ((), ())), preferred_element_type=F32
    )
    same = (iota((tall, tall), 0) % group) == (iota((tall, tall), 1) % group)
    occ_wide = jnp.where(same, wide, 0.0).astype(BF16)
    four = 4
    side = four * width
    repeat = jnp.where(iota((side, width), 0) % width == iota((side, width), 1), 1.0, 0.0).astype(BF16)
    rows = jnp.dot(repeat, virt_ref[0], preferred_element_type=F32).astype(BF16)
    wide = lax.dot_general(
        rows, repeat, (((1,), (1,)), ((), ())), preferred_element_type=F32
    )
    same = (iota((side, side), 0) // width) == (iota((side, side), 1) // width)
    virt_wide = jnp.where(same, wide, 0.0).astype(BF16)

    tiles = tiles_ref.reshape(width, width, cols)
    for t in range(width // group):
        part = tiles[:, t * group : (t + 1) * group, :].reshape(tall, cols)
        half = jnp.dot(occ_wide, part, preferred_element_type=F32).astype(BF16)
        half_ref[:, t * group : (t + 1) * group, :] = half.reshape(width, group, cols)
    weight = jnp.where(iota((1, cols), 1) < HALF, scalars[2], scalars[3]).astype(F32)
    for g in range(width // four):
        part = half_ref[g * four : (g + 1) * four].reshape(side, cols)
        done = jnp.dot(virt_wide, part, preferred_element_type=F32) * weight
        out_ref[g * side : (g + 1) * side, :] = done.astype(BF16)


def contract(scalars, three_centre, green_occ, green_virt):
    width = green_occ.shape[1]
    rows, cols = three_centre.shape
    whole = pl.BlockSpec((rows, cols), lambda i, s: (0, 0))
    return pl.pallas_call(
        functools.partial(contract_kernel, width, 16),
        grid_spec=pltpu.PrefetchScalarGridSpec(
            num_scalar_prefetch=1,
            grid=(1,),
            in_specs=[
                whole,
                pl.BlockSpec((1, width, width), lambda i, s: (s[0], 0, 0)),
                pl.BlockSpec((1, width, width), lambda i, s: (s[1], 0, 0)),
            ],
            out_specs=whole,
            scratch_shapes=[pltpu.VMEM((width, width, cols), BF16)],
        ),
        out_shape=jax.ShapeDtypeStruct((rows, cols), BF16),
        compiler_params=pltpu.CompilerParams(vmem_limit_bytes=40 * 2**20),
        cost_estimate=pl.CostEstimate(
            flops=40 * 10**9, bytes_accessed=4 * 2**20, transcendentals=0
        ),
    )(scalars, three_centre, green_occ, green_virt)


def products_kernel(steps, pairs, has_far, scalars, *refs):
    per_side = 5 if has_far else 3
    a_refs, b_refs = refs[:per_side], refs[per_side : 2 * per_side]
    keep_ref, send_ref, acc = refs[2 * per_side :]
    k = pl.program_id(0)
    core = scalars[4]

    @pl.when(k == 0)
    def _():
        acc[...] = jnp.zeros_like(acc)

    def block(blocks, offset):
        if offset == 2:
            return jnp.where(k < steps // 2, blocks[3][...], blocks[4][...])
        return blocks[NEAR.index(offset)][...]

    rights = {q: block(b_refs, q) for q in sorted({q for _, q in pairs})}
    for p in sorted({p for p, _ in pairs}):
        left = block(a_refs, p).T
        for i, (task_p, q) in enumerate(pairs):
            if task_p == p:
                acc[i] += jnp.dot(left, rights[q], preferred_element_type=F32)

    @pl.when(k == steps - 1)
    def _():
        for i, (p, _) in enumerate(pairs):
            for half in range(2):
                rows = pl.ds(half * HALF, HALF)
                acc[i, rows, :] = acc[i, rows, :] * scalars[8 + 2 * p + half].astype(F32)
            keep_ref[i] = acc[i, pl.ds(pl.multiple_of(core * HALF, HALF), HALF), :]
            other = pl.ds(pl.multiple_of((1 - core) * HALF, HALF), HALF)
            send_ref[i] = acc[i, other, :].astype(BF16)


def products(scalars, lefts, rights, pairs):
    rows = lefts[0].shape[0]
    chunk = 1024
    steps = rows // chunk
    has_far = len(lefts) == 5
    specs = [pl.BlockSpec((chunk, BLOCK), lambda k, s: (k, 0))] * 3
    if has_far:
        specs.append(
            pl.BlockSpec((chunk, BLOCK), lambda k, s: (jnp.minimum(k, steps // 2 - 1), 0))
        )
        specs.append(
            pl.BlockSpec((chunk, BLOCK), lambda k, s: (jnp.maximum(k - steps // 2, 0), 0))
        )
    count = len(pairs)
    out = pl.BlockSpec((count, HALF, BLOCK), lambda k, s: (0, 0, 0))
    return pl.pallas_call(
        functools.partial(products_kernel, steps, pairs, has_far),
        grid_spec=pltpu.PrefetchScalarGridSpec(
            num_scalar_prefetch=1,
            grid=(steps,),
            in_specs=specs + specs,
            out_specs=[out, out],
            scratch_shapes=[pltpu.VMEM((count, BLOCK, BLOCK), F32)],
        ),
        out_shape=[
            jax.ShapeDtypeStruct((count, HALF, BLOCK), F32),
            jax.ShapeDtypeStruct((count, HALF, BLOCK), BF16),
        ],
        compiler_params=pltpu.CompilerParams(vmem_limit_bytes=48 * 2**20),
        cost_estimate=pl.CostEstimate(
            flops=2 * count * rows * BLOCK * BLOCK, bytes_accessed=20 * 2**20, transcendentals=0
        ),
    )(scalars, *lefts, *rights)


def merge_kernel(near, far, scalars, *refs):
    keep_near, got_near, keep_far, got_far = refs[:4]
    out_refs = refs[4:]
    own_ref, send_refs = out_refs[0], out_refs[1:]

    for pairs, keep, got in ((near, keep_near, got_near), (far, keep_far, got_far)):
        for i, (p, q) in enumerate(pairs):
            total = keep[i] + got[i].astype(F32)
            target = scalars[16 + q]
            row = scalars[20 + p]

            @pl.when(target == 0)
            def _():
                own_ref[row] = total

            for step in range(1, SIDE):

                @pl.when(target == step)
                def _():
                    send_refs[step - 1][row] = total.astype(BF16)


def merge(scalars, near, far, keep_near, got_near, keep_far, got_far):
    shape = (SIDE, HALF, BLOCK)
    spec = lambda n: pl.BlockSpec((n, HALF, BLOCK), lambda i, s: (0, 0, 0))
    return pl.pallas_call(
        functools.partial(merge_kernel, near, far),
        grid_spec=pltpu.PrefetchScalarGridSpec(
            num_scalar_prefetch=1,
            grid=(1,),
            in_specs=[spec(len(near))] * 2 + [spec(len(far))] * 2,
            out_specs=[spec(SIDE)] * 4,
        ),
        out_shape=[jax.ShapeDtypeStruct(shape, F32)] + [jax.ShapeDtypeStruct(shape, BF16)] * 3,
        compiler_params=pltpu.CompilerParams(vmem_limit_bytes=32 * 2**20),
        cost_estimate=pl.CostEstimate(flops=2**20, bytes_accessed=5 * 2**20, transcendentals=0),
    )(scalars, keep_near, got_near, keep_far, got_far)


def ring(block, axis):
    take_next = [((i + 1) % SIDE, i) for i in range(SIDE)]
    take_prev = [((i - 1) % SIDE, i) for i in range(SIDE)]
    return lax.ppermute(block, axis, take_next), lax.ppermute(block, axis, take_prev)


def far(after, before, axis):
    half = after.shape[0] // 2
    take_next = [((i + 1) % SIDE, i) for i in range(SIDE)]
    take_prev = [((i - 1) % SIDE, i) for i in range(SIDE)]
    return (
        lax.ppermute(after[:half], axis, take_next),
        lax.ppermute(before[half:], axis, take_prev),
    )


def per_device(three_centre, tile_list, pair_blocks, green_occ, green_virt):
    y, c, z, x = (lax.axis_index(name) for name in ("y", "c", "z", "x"))
    offsets = jnp.arange(SIDE)
    a_after, a_before = ring(three_centre, "x")
    own = contract(
        jnp.concatenate([pair_blocks[0], tile_list[0]]), three_centre, green_occ, green_virt
    )
    b_after, b_before = ring(own, "z")
    listed, own = lax.optimization_barrier((tile_list, own))
    row_weights = lax.all_gather(listed[0], "x")
    row_weights = jnp.take(row_weights, (x + offsets) & 3, axis=0).reshape(-1)
    first = 2 * (x & 1) + c
    scalars = jnp.concatenate(
        [
            jnp.stack([y, z, x, c, c, c, c, c]),
            row_weights,
            (z + offsets - y) & 3,
            (x + offsets - first) & 3,
        ]
    ).astype(jnp.int32)

    near = tuple((p, q) for p in NEAR for q in NEAR)
    lefts, rights = [three_centre, a_after, a_before], [own, b_after, b_before]
    keep_near, send_near = products(scalars, lefts, rights, near)
    lefts += far(a_after, a_before, "x")
    rights += far(b_after, b_before, "z")
    swap = [(0, 1), (1, 0)]
    got_near = lax.ppermute(send_near, "c", swap)
    keep_far, send_far = products(scalars, lefts, rights, LATE)
    got_far = lax.ppermute(send_far, "c", swap)

    own, *sends = merge(scalars, near, LATE, keep_near, got_near, keep_far, got_far)
    for k in range(1, SIDE):
        moved = lax.ppermute(sends[k - 1], "y", [(i, (i + k) % SIDE) for i in range(SIDE)])
        own = own + moved.astype(F32)
    own = -2.0 * own

    arrived = []
    for k in range(SIDE):
        perm = [
            (core * SIDE + i, (i // 2) * SIDE + (2 * (i % 2) + core + k) % SIDE)
            for core in range(2)
            for i in range(SIDE)
        ]
        arrived.append(lax.ppermute(own[k], ("c", "x"), perm))
    stacked = jnp.stack(arrived[::-1] + arrived[:0:-1])
    ordered = lax.dynamic_slice_in_dim(stacked, (SIDE - 1 - x) & 3, SIDE, 0)
    ordered = ordered.reshape(2, 2, HALF, BLOCK)
    return ordered.transpose(1, 2, 0, 3).reshape(BLOCK, 2 * BLOCK)


def solution(mesh):
    fine = Mesh(mesh.devices.reshape(SIDE, 2, SIDE, SIDE), ("y", "c", "z", "x"))
    ao, aux = ("y", "c"), ("z", "x")
    return jax.shard_map(
        per_device,
        mesh=fine,
        in_specs=(P(ao, aux), P(ao, aux), P(ao, None), P(), P()),
        out_specs=P(aux, ao),
        check_vma=False,
    )
```

```python
import functools

import jax
import jax.numpy as jnp
from jax import lax
from jax.experimental import pallas as pl
from jax.experimental.pallas import tpu as pltpu
from jax.sharding import Mesh, PartitionSpec as P

SIDE = 4
BLOCK = 256
HALF = BLOCK // 2
NEAR = (0, 1, 3)
LATE = tuple((2, q) for q in NEAR + (2,)) + tuple((p, 2) for p in NEAR)
F32 = jnp.float32
BF16 = jnp.bfloat16


def iota(shape, dim):
    return lax.broadcasted_iota(jnp.int32, shape, dim)


def contract_kernel(width, group, scalars, tiles_ref, occ_ref, virt_ref, out_ref, masked_ref, half_ref):
    cols = tiles_ref.shape[1]
    tall = width * group
    spread = jnp.where(iota((tall, width), 0) // group == iota((tall, width), 1), 1.0, 0.0).astype(BF16)
    rows = jnp.dot(spread, occ_ref[0], preferred_element_type=F32).astype(BF16)
    wide = lax.dot_general(
        rows, spread, (((1,), (1,)), ((), ())), preferred_element_type=F32
    )
    same = (iota((tall, tall), 0) % group) == (iota((tall, tall), 1) % group)
    occ_wide = jnp.where(same, wide, 0.0).astype(BF16)
    four = 4
    side = four * width
    repeat = jnp.where(iota((side, width), 0) % width == iota((side, width), 1), 1.0, 0.0).astype(BF16)
    rows = jnp.dot(repeat, virt_ref[0], preferred_element_type=F32).astype(BF16)
    wide = lax.dot_general(
        rows, repeat, (((1,), (1,)), ((), ())), preferred_element_type=F32
    )
    same = (iota((side, side), 0) // width) == (iota((side, side), 1) // width)
    virt_wide = jnp.where(same, wide, 0.0).astype(BF16)

    tiles = tiles_ref.reshape(width, width, cols)
    for t in range(width // group):
        part = tiles[:, t * group : (t + 1) * group, :].reshape(tall, cols)
        half = jnp.dot(occ_wide, part, preferred_element_type=F32).astype(BF16)
        half_ref[:, t * group : (t + 1) * group, :] = half.reshape(width, group, cols)
    weight = jnp.where(iota((1, cols), 1) < HALF, scalars[2], scalars[3]).astype(F32)
    for g in range(width // four):
        part = half_ref[g * four : (g + 1) * four].reshape(side, cols)
        done = jnp.dot(virt_wide, part, preferred_element_type=F32) * weight
        rows = slice(g * side, (g + 1) * side)
        out_ref[rows, :] = done.astype(BF16)
        masked_ref[rows, :] = tiles_ref[rows, :] * weight.astype(BF16)


def contract(scalars, three_centre, green_occ, green_virt):
    width = green_occ.shape[1]
    rows, cols = three_centre.shape
    whole = pl.BlockSpec((rows, cols), lambda i, s: (0, 0))
    return pl.pallas_call(
        functools.partial(contract_kernel, width, 16),
        grid_spec=pltpu.PrefetchScalarGridSpec(
            num_scalar_prefetch=1,
            grid=(1,),
            in_specs=[
                whole,
                pl.BlockSpec((1, width, width), lambda i, s: (s[0], 0, 0)),
                pl.BlockSpec((1, width, width), lambda i, s: (s[1], 0, 0)),
            ],
            out_specs=[whole, whole],
            scratch_shapes=[pltpu.VMEM((width, width, cols), BF16)],
        ),
        out_shape=[jax.ShapeDtypeStruct((rows, cols), BF16)] * 2,
        compiler_params=pltpu.CompilerParams(vmem_limit_bytes=60 * 2**20),
        cost_estimate=pl.CostEstimate(
            flops=40 * 10**9, bytes_accessed=4 * 2**20, transcendentals=0
        ),
    )(scalars, three_centre, green_occ, green_virt)


def products_kernel(steps, pairs, has_far, scalars, *refs):
    per_side = 5 if has_far else 3
    a_refs, b_refs = refs[:per_side], refs[per_side : 2 * per_side]
    keep_ref, send_ref, acc = refs[2 * per_side :]
    k = pl.program_id(0)
    core = scalars[8]

    @pl.when(k == 0)
    def _():
        acc[...] = jnp.zeros_like(acc)

    def block(blocks, offset):
        if offset == 2:
            return jnp.where(k < steps // 2, blocks[3][...], blocks[4][...])
        return blocks[NEAR.index(offset)][...]

    rights = {q: block(b_refs, q) for q in sorted({q for _, q in pairs})}
    for p in sorted({p for p, _ in pairs}):
        left = block(a_refs, p).T
        for i, (task_p, q) in enumerate(pairs):
            if task_p == p:
                acc[i] += jnp.dot(left, rights[q], preferred_element_type=F32)

    @pl.when(k == steps - 1)
    def _():
        for i in range(len(pairs)):
            keep_ref[i] = acc[i, pl.ds(pl.multiple_of(core * HALF, HALF), HALF), :]
            other = pl.ds(pl.multiple_of((1 - core) * HALF, HALF), HALF)
            send_ref[i] = acc[i, other, :].astype(BF16)


def products(scalars, lefts, rights, pairs):
    rows = lefts[0].shape[0]
    chunk = 1024
    steps = rows // chunk
    has_far = len(lefts) == 5
    specs = [pl.BlockSpec((chunk, BLOCK), lambda k, s: (k, 0))] * 3
    if has_far:
        specs.append(
            pl.BlockSpec((chunk, BLOCK), lambda k, s: (jnp.minimum(k, steps // 2 - 1), 0))
        )
        specs.append(
            pl.BlockSpec((chunk, BLOCK), lambda k, s: (jnp.maximum(k - steps // 2, 0), 0))
        )
    count = len(pairs)
    out = pl.BlockSpec((count, HALF, BLOCK), lambda k, s: (0, 0, 0))
    return pl.pallas_call(
        functools.partial(products_kernel, steps, pairs, has_far),
        grid_spec=pltpu.PrefetchScalarGridSpec(
            num_scalar_prefetch=1,
            grid=(steps,),
            in_specs=specs + specs,
            out_specs=[out, out],
            scratch_shapes=[pltpu.VMEM((count, BLOCK, BLOCK), F32)],
        ),
        out_shape=[
            jax.ShapeDtypeStruct((count, HALF, BLOCK), F32),
            jax.ShapeDtypeStruct((count, HALF, BLOCK), BF16),
        ],
        compiler_params=pltpu.CompilerParams(vmem_limit_bytes=(24 if has_far else 20) * 2**20),
        cost_estimate=pl.CostEstimate(
            flops=2 * count * rows * BLOCK * BLOCK, bytes_accessed=20 * 2**20, transcendentals=0
        ),
    )(scalars, *lefts, *rights)


def merge_kernel(near, far, scalars, *refs):
    keep_near, got_near, keep_far, got_far, out_ref = refs
    for pairs, keep, got in ((near, keep_near, got_near), (far, keep_far, got_far)):
        for i, (p, q) in enumerate(pairs):
            target = scalars[SIDE + q] * SIDE + scalars[p]
            out_ref[target] = (keep[i] + got[i].astype(F32)).astype(BF16)


def merge(scalars, near, far, keep_near, got_near, keep_far, got_far):
    spec = lambda n: pl.BlockSpec((n, HALF, BLOCK), lambda i, s: (0, 0, 0))
    return pl.pallas_call(
        functools.partial(merge_kernel, near, far),
        grid_spec=pltpu.PrefetchScalarGridSpec(
            num_scalar_prefetch=1,
            grid=(1,),
            in_specs=[spec(len(near))] * 2 + [spec(len(far))] * 2,
            out_specs=spec(SIDE * SIDE),
        ),
        out_shape=jax.ShapeDtypeStruct((SIDE * SIDE, HALF, BLOCK), BF16),
        compiler_params=pltpu.CompilerParams(vmem_limit_bytes=24 * 2**20),
        cost_estimate=pl.CostEstimate(flops=2**20, bytes_accessed=5 * 2**20, transcendentals=0),
    )(scalars, keep_near, got_near, keep_far, got_far)


def total_kernel(scalars, parts_ref, mine_ref, theirs_ref):
    core = scalars[8]
    for j in range(2):
        for out_ref, base in ((mine_ref, 2 * core), (theirs_ref, 2 * (1 - core))):
            added = parts_ref[base + j].astype(F32)
            for y in range(1, SIDE):
                added += parts_ref[y * SIDE + base + j].astype(F32)
            out_ref[j] = -2.0 * added


def total(scalars, parts):
    return pl.pallas_call(
        total_kernel,
        grid_spec=pltpu.PrefetchScalarGridSpec(
            num_scalar_prefetch=1,
            grid=(1,),
            in_specs=[pl.BlockSpec(parts.shape, lambda i, s: (0, 0, 0))],
            out_specs=[pl.BlockSpec((2, HALF, BLOCK), lambda i, s: (0, 0, 0))] * 2,
        ),
        out_shape=[jax.ShapeDtypeStruct((2, HALF, BLOCK), F32)] * 2,
        compiler_params=pltpu.CompilerParams(vmem_limit_bytes=16 * 2**20),
        cost_estimate=pl.CostEstimate(flops=2**20, bytes_accessed=2 * 2**20, transcendentals=0),
    )(scalars, parts)


def place_kernel(scalars, mine_ref, other_ref, out_ref):
    core = scalars[8]
    for in_ref, half in ((mine_ref, core), (other_ref, 1 - core)):
        rows = pl.ds(pl.multiple_of(half * HALF, HALF), HALF)
        for j in range(2):
            out_ref[rows, j * BLOCK : (j + 1) * BLOCK] = in_ref[j]


def place(scalars, mine, other):
    spec = pl.BlockSpec((2, HALF, BLOCK), lambda i, s: (0, 0, 0))
    return pl.pallas_call(
        place_kernel,
        grid_spec=pltpu.PrefetchScalarGridSpec(
            num_scalar_prefetch=1,
            grid=(1,),
            in_specs=[spec, spec],
            out_specs=pl.BlockSpec((BLOCK, 2 * BLOCK), lambda i, s: (0, 0)),
        ),
        out_shape=jax.ShapeDtypeStruct((BLOCK, 2 * BLOCK), F32),
        compiler_params=pltpu.CompilerParams(vmem_limit_bytes=16 * 2**20),
        cost_estimate=pl.CostEstimate(flops=2**18, bytes_accessed=2**20, transcendentals=0),
    )(scalars, mine, other)


def ring(block, axis):
    take_next = [((i + 1) % SIDE, i) for i in range(SIDE)]
    take_prev = [((i - 1) % SIDE, i) for i in range(SIDE)]
    return lax.ppermute(block, axis, take_next), lax.ppermute(block, axis, take_prev)


def far(after, before, axis):
    half = after.shape[0] // 2
    take_next = [((i + 1) % SIDE, i) for i in range(SIDE)]
    take_prev = [((i - 1) % SIDE, i) for i in range(SIDE)]
    return (
        lax.ppermute(after[:half], axis, take_next),
        lax.ppermute(before[half:], axis, take_prev),
    )


def per_device(three_centre, tile_list, pair_blocks, green_occ, green_virt):
    y, c, z, x = (lax.axis_index(name) for name in ("y", "c", "z", "x"))
    offsets = jnp.arange(SIDE)
    scalars = jnp.concatenate([(x + offsets) & 3, (z + offsets) & 3, c[None]]).astype(jnp.int32)
    own, masked = contract(
        jnp.concatenate([pair_blocks[0], tile_list[0]]), three_centre, green_occ, green_virt
    )
    b_after, b_before = ring(own, "z")
    a_after, a_before = ring(masked, "x")

    near = tuple((p, q) for p in NEAR for q in NEAR)
    lefts, rights = [masked, a_after, a_before], [own, b_after, b_before]
    keep_near, send_near = products(scalars, lefts, rights, near)
    rights += far(b_after, b_before, "z")
    lefts += far(a_after, a_before, "x")
    swap = [(0, 1), (1, 0)]
    got_near = lax.ppermute(send_near, "c", swap)
    keep_far, send_far = products(scalars, lefts, rights, LATE)
    got_far = lax.ppermute(send_far, "c", swap)

    sends = merge(scalars, near, LATE, keep_near, got_near, keep_far, got_far)
    parts = lax.all_to_all(sends, ("y", "x"), 0, 0)
    mine, theirs = total(scalars, parts)
    return place(scalars, mine, lax.ppermute(theirs, "c", swap))


def solution(mesh):
    fine = Mesh(mesh.devices.reshape(SIDE, 2, SIDE, SIDE), ("y", "c", "z", "x"))
    ao, aux = ("y", "c"), ("z", "x")
    return jax.shard_map(
        per_device,
        mesh=fine,
        in_specs=(P(ao, aux), P(ao, aux), P(ao, None), P(), P()),
        out_specs=P(aux, ao),
        check_vma=False,
    )
```

```python
import functools

import jax
import jax.numpy as jnp
from jax import lax
from jax.experimental import pallas as pl
from jax.experimental.pallas import tpu as pltpu
from jax.sharding import Mesh, PartitionSpec as P

SIDE = 4
BLOCK = 256
HALF = BLOCK // 2
GROUPS = (
    ((0, 0), (1, 0), (3, 0)),
    ((0, 1), (1, 1), (3, 1), (0, 3), (1, 3), (3, 3)),
    ((2, 0), (2, 1), (2, 3), (0, 2), (1, 2), (3, 2), (2, 2)),
)
COSTS = (10, 1, 1)
F32 = jnp.float32
BF16 = jnp.bfloat16


def iota(shape, dim):
    return lax.broadcasted_iota(jnp.int32, shape, dim)


def contract_kernel(width, group, pairs, tiles_ref, occ_ref, virt_ref, low_ref, high_ref, half_ref):
    cols = tiles_ref.shape[1]
    tall = width * group
    spread = jnp.where(iota((width, tall), 1) // group == iota((width, tall), 0), 1.0, 0.0)
    wide = jnp.dot(occ_ref[0], spread.astype(BF16), preferred_element_type=F32).astype(BF16)
    same = iota((group, tall), 0) == iota((group, tall), 1) % group
    same = jnp.where(same, 1.0, 0.0).astype(BF16)
    occ_wide = (wide[:, None, :] * same[None]).reshape(tall, tall)
    four = 4
    side = four * width
    spread = jnp.where(iota((width, side), 1) % width == iota((width, side), 0), 1.0, 0.0)
    wide = jnp.dot(virt_ref[0], spread.astype(BF16), preferred_element_type=F32)
    same = iota((side, side), 0) // width == iota((side, side), 1) // width
    virt_wide = jnp.where(same, jnp.concatenate([wide] * four), 0.0).astype(BF16)

    tiles = tiles_ref.reshape(width, width, cols)
    for t in range(width // group):
        part = tiles[:, t * group : (t + 1) * group, :].reshape(tall, cols)
        half = jnp.dot(occ_wide, part, preferred_element_type=F32).astype(BF16)
        half_ref[:, t * group : (t + 1) * group, :] = half.reshape(width, group, cols)
    for g in range(width // four):
        part = half_ref[g * four : (g + 1) * four].reshape(side, cols)
        done = jnp.dot(virt_wide, part, preferred_element_type=F32).astype(BF16)
        out_ref, h = (low_ref, g) if g < width // 8 else (high_ref, g - width // 8)
        out_ref[h * side : (h + 1) * side, :] = done


def contract(pairs, tiles, green_occ, green_virt):
    width = green_occ.shape[1]
    rows, cols = tiles.shape
    whole = pl.BlockSpec((rows, cols), lambda i, s: (0, 0))
    return pl.pallas_call(
        functools.partial(contract_kernel, width, 16),
        grid_spec=pltpu.PrefetchScalarGridSpec(
            num_scalar_prefetch=1,
            grid=(1,),
            in_specs=[
                whole,
                pl.BlockSpec((1, width, width), lambda i, s: (s[0, 0], 0, 0)),
                pl.BlockSpec((1, width, width), lambda i, s: (s[0, 1], 0, 0)),
            ],
            out_specs=[pl.BlockSpec((rows // 2, cols), lambda i, s: (0, 0))] * 2,
            scratch_shapes=[pltpu.VMEM((width, width, cols), BF16)],
        ),
        out_shape=[jax.ShapeDtypeStruct((rows // 2, cols), BF16)] * 2,
        compiler_params=pltpu.CompilerParams(vmem_limit_bytes=24 * 2**20),
        cost_estimate=pl.CostEstimate(
            flops=40 * 10**9, bytes_accessed=4 * 2**20, transcendentals=0
        ),
    )(pairs, tiles, green_occ, green_virt)


def products_kernel(steps, pairs, left_at, right_at, scalars, *refs):
    keep_ref, send_ref, acc = refs[-3:]
    k = pl.program_id(0)
    core = scalars[8]

    @pl.when(k == 0)
    def _():
        acc[...] = jnp.zeros_like(acc)

    def step(second):
        rights = {q: refs[places[second % len(places)]][...] for q, places in right_at.items()}
        for p, places in left_at.items():
            left = refs[places[second % len(places)]][...].T
            for i, (task_p, q) in enumerate(pairs):
                if task_p == p:
                    acc[i] += jnp.dot(left, rights[q], preferred_element_type=F32)

    @pl.when(k < steps // 2)
    def _():
        step(0)

    @pl.when(k >= steps // 2)
    def _():
        step(1)

    @pl.when(k == steps - 1)
    def _():
        for i in range(len(pairs)):
            keep_ref[i] = acc[i, pl.ds(pl.multiple_of(core * HALF, HALF), HALF), :]
            other = pl.ds(pl.multiple_of((1 - core) * HALF, HALF), HALF)
            send_ref[i] = acc[i, other, :].astype(BF16)


def products(scalars, lefts, rights, pairs, cost, after):
    rows = sum(half.shape[0] for half in lefts[pairs[0][0]])
    chunk = 1024
    steps = rows // chunk
    operands, specs = [], []

    def places(blocks):
        first = len(operands)
        for half, array in enumerate(blocks):
            operands.append(array)
            if len(blocks) == 1:
                index = lambda k, s: (k, 0)
            elif half == 0:
                index = lambda k, s: (jnp.minimum(k, steps // 2 - 1), 0)
            else:
                index = lambda k, s: (jnp.maximum(k - steps // 2, 0), 0)
            specs.append(pl.BlockSpec((chunk, BLOCK), index))
        return tuple(range(first, len(operands)))

    left_at = {p: places(lefts[p]) for p in sorted({p for p, _ in pairs})}
    right_at = {q: places(rights[q]) for q in sorted({q for _, q in pairs})}
    for array in after:
        operands.append(array)
        specs.append(pl.BlockSpec(memory_space=pl.ANY))
    count = len(pairs)
    out = pl.BlockSpec((count, HALF, BLOCK), lambda k, s: (0, 0, 0))
    return pl.pallas_call(
        functools.partial(products_kernel, steps, pairs, left_at, right_at),
        grid_spec=pltpu.PrefetchScalarGridSpec(
            num_scalar_prefetch=1,
            grid=(steps,),
            in_specs=specs,
            out_specs=[out, out],
            scratch_shapes=[pltpu.VMEM((count, BLOCK, BLOCK), F32)],
        ),
        out_shape=[
            jax.ShapeDtypeStruct((count, HALF, BLOCK), F32),
            jax.ShapeDtypeStruct((count, HALF, BLOCK), BF16),
        ],
        compiler_params=pltpu.CompilerParams(vmem_limit_bytes=16 * 2**20),
        cost_estimate=pl.CostEstimate(
            flops=cost * 2 * count * rows * BLOCK * BLOCK,
            bytes_accessed=2**20,
            transcendentals=0,
        ),
    )(scalars, *operands)


def merge_kernel(groups, scalars, *refs):
    out_ref = refs[-1]
    for n, pairs in enumerate(groups):
        keep, got = refs[2 * n], refs[2 * n + 1]
        for i, (p, q) in enumerate(pairs):
            target = scalars[SIDE + q] * SIDE + scalars[p]
            out_ref[target] = (keep[i] + got[i].astype(F32)).astype(BF16)


def merge(scalars, groups, halves):
    spec = lambda n: pl.BlockSpec((n, HALF, BLOCK), lambda i, s: (0, 0, 0))
    return pl.pallas_call(
        functools.partial(merge_kernel, groups),
        grid_spec=pltpu.PrefetchScalarGridSpec(
            num_scalar_prefetch=1,
            grid=(1,),
            in_specs=[spec(len(pairs)) for pairs in groups for _ in range(2)],
            out_specs=spec(SIDE * SIDE),
        ),
        out_shape=jax.ShapeDtypeStruct((SIDE * SIDE, HALF, BLOCK), BF16),
        compiler_params=pltpu.CompilerParams(vmem_limit_bytes=24 * 2**20),
        cost_estimate=pl.CostEstimate(flops=2**20, bytes_accessed=5 * 2**20, transcendentals=0),
    )(scalars, *halves)


def added(core, parts_ref, j):
    total = parts_ref[2 * core + j].astype(F32)
    for y in range(1, SIDE):
        total += parts_ref[y * SIDE + 2 * core + j].astype(F32)
    return -2.0 * total


def theirs_kernel(scalars, parts_ref, out_ref):
    for j in range(2):
        out_ref[j] = added(1 - scalars[8], parts_ref, j)


def theirs(scalars, parts):
    return pl.pallas_call(
        theirs_kernel,
        grid_spec=pltpu.PrefetchScalarGridSpec(
            num_scalar_prefetch=1,
            grid=(1,),
            in_specs=[pl.BlockSpec(parts.shape, lambda i, s: (0, 0, 0))],
            out_specs=pl.BlockSpec((2, HALF, BLOCK), lambda i, s: (0, 0, 0)),
        ),
        out_shape=jax.ShapeDtypeStruct((2, HALF, BLOCK), F32),
        compiler_params=pltpu.CompilerParams(vmem_limit_bytes=16 * 2**20),
        cost_estimate=pl.CostEstimate(flops=2**20, bytes_accessed=2 * 2**20, transcendentals=0),
    )(scalars, parts)


def place_kernel(scalars, parts_ref, other_ref, out_ref):
    core = scalars[8]
    own = pl.ds(pl.multiple_of(core * HALF, HALF), HALF)
    rest = pl.ds(pl.multiple_of((1 - core) * HALF, HALF), HALF)
    for j in range(2):
        out_ref[own, j * BLOCK : (j + 1) * BLOCK] = added(core, parts_ref, j)
        out_ref[rest, j * BLOCK : (j + 1) * BLOCK] = other_ref[j]


def place(scalars, parts, other):
    return pl.pallas_call(
        place_kernel,
        grid_spec=pltpu.PrefetchScalarGridSpec(
            num_scalar_prefetch=1,
            grid=(1,),
            in_specs=[
                pl.BlockSpec(parts.shape, lambda i, s: (0, 0, 0)),
                pl.BlockSpec((2, HALF, BLOCK), lambda i, s: (0, 0, 0)),
            ],
            out_specs=pl.BlockSpec((BLOCK, 2 * BLOCK), lambda i, s: (0, 0)),
        ),
        out_shape=jax.ShapeDtypeStruct((BLOCK, 2 * BLOCK), F32),
        compiler_params=pltpu.CompilerParams(vmem_limit_bytes=16 * 2**20),
        cost_estimate=pl.CostEstimate(flops=2**18, bytes_accessed=2**20, transcendentals=0),
    )(scalars, parts, other)


def ring(block, axis):
    take_next = [((i + 1) % SIDE, i) for i in range(SIDE)]
    take_prev = [((i - 1) % SIDE, i) for i in range(SIDE)]
    return lax.ppermute(block, axis, take_next), lax.ppermute(block, axis, take_prev)


def far(after, before, axis):
    half = after.shape[0] // 2
    take_next = [((i + 1) % SIDE, i) for i in range(SIDE)]
    take_prev = [((i - 1) % SIDE, i) for i in range(SIDE)]
    return (
        lax.ppermute(after[:half], axis, take_next),
        lax.ppermute(before[half:], axis, take_prev),
    )


def around(low, high, axis):
    take_next = [((i + 1) % SIDE, i) for i in range(SIDE)]
    take_prev = [((i - 1) % SIDE, i) for i in range(SIDE)]
    after_low = lax.ppermute(low, axis, take_next)
    before_high = lax.ppermute(high, axis, take_prev)
    after_high = lax.ppermute(high, axis, take_next)
    before_low = lax.ppermute(low, axis, take_prev)
    far_low = lax.ppermute(after_low, axis, take_next)
    far_high = lax.ppermute(before_high, axis, take_prev)
    return {
        0: (low, high),
        1: (after_low, after_high),
        3: (before_low, before_high),
        2: (far_low, far_high),
    }


def per_device(three_centre, tile_list, pair_blocks, green_occ, green_virt):
    y, c, z, x = (lax.axis_index(name) for name in ("y", "c", "z", "x"))
    offsets = jnp.arange(SIDE)
    scalars = jnp.concatenate([(x + offsets) & 3, (z + offsets) & 3, c[None]]).astype(jnp.int32)
    weights = jnp.repeat(tile_list[0].astype(BF16), BLOCK // tile_list.shape[1])
    masked = three_centre * weights[None, :]
    a_after, a_before = ring(masked, "x")
    rights = around(*contract(pair_blocks, masked, green_occ, green_virt), "z")
    lefts = {0: (masked,), 1: (a_after,), 3: (a_before,), 2: far(a_after, a_before, "x")}

    swap = [(0, 1), (1, 0)]
    halves = []
    for pairs, cost in zip(GROUPS, COSTS):
        keep, send = products(scalars, lefts, rights, pairs, cost, halves[-2:-1])
        halves += [keep, lax.ppermute(send, "c", swap)]
    sends = merge(scalars, GROUPS, halves)
    parts = lax.all_to_all(sends, ("y", "x"), 0, 0)
    return place(scalars, parts, lax.ppermute(theirs(scalars, parts), "c", swap))


def solution(mesh):
    fine = Mesh(mesh.devices.reshape(SIDE, 2, SIDE, SIDE), ("y", "c", "z", "x"))
    ao, aux = ("y", "c"), ("z", "x")
    return jax.shard_map(
        per_device,
        mesh=fine,
        in_specs=(P(ao, aux), P(ao, aux), P(ao, None), P(), P()),
        out_specs=P(aux, ao),
        check_vma=False,
    )
```

```python
import functools

import jax
import jax.numpy as jnp
from jax import lax
from jax.experimental import pallas as pl
from jax.experimental.pallas import tpu as pltpu
from jax.sharding import Mesh, PartitionSpec as P

SIDE = 4
BLOCK = 256
HALF = BLOCK // 2
GROUPS = (
    ((0, 0), (1, 0), (3, 0)),
    ((0, 1), (1, 1), (3, 1), (0, 3), (1, 3), (3, 3)),
    ((2, 0), (2, 1), (2, 3), (0, 2), (1, 2), (3, 2), (2, 2)),
)
COSTS = (10, 1, 1)
NEAR = (0, 1, 3)
LIMIT = 12
IN_VMEM = pl.BlockSpec(memory_space=pltpu.VMEM)
IN_SMEM = pl.BlockSpec(memory_space=pltpu.SMEM)
F32 = jnp.float32
BF16 = jnp.bfloat16


def iota(shape, dim):
    return lax.broadcasted_iota(jnp.int32, shape, dim)


def contract_kernel(width, group, pairs, tiles_ref, occ_ref, virt_ref, low_ref, high_ref, half_ref):
    cols = tiles_ref.shape[1]
    tall = width * group
    spread = jnp.where(iota((width, tall), 1) // group == iota((width, tall), 0), 1.0, 0.0)
    wide = jnp.dot(occ_ref[pairs[0, 0]], spread.astype(BF16), preferred_element_type=F32).astype(BF16)
    same = iota((group, tall), 0) == iota((group, tall), 1) % group
    same = jnp.where(same, 1.0, 0.0).astype(BF16)
    occ_wide = (wide[:, None, :] * same[None]).reshape(tall, tall)
    four = 4
    side = four * width
    spread = jnp.where(iota((width, side), 1) % width == iota((width, side), 0), 1.0, 0.0)
    wide = jnp.dot(virt_ref[pairs[0, 1]], spread.astype(BF16), preferred_element_type=F32)
    same = iota((side, side), 0) // width == iota((side, side), 1) // width
    virt_wide = jnp.where(same, jnp.concatenate([wide] * four), 0.0).astype(BF16)

    tiles = tiles_ref.reshape(width, width, cols)
    for t in range(width // group):
        part = tiles[:, t * group : (t + 1) * group, :].reshape(tall, cols)
        half = jnp.dot(occ_wide, part, preferred_element_type=F32).astype(BF16)
        half_ref[:, t * group : (t + 1) * group, :] = half.reshape(width, group, cols)
    for g in range(width // four):
        part = half_ref[g * four : (g + 1) * four].reshape(side, cols)
        done = jnp.dot(virt_wide, part, preferred_element_type=F32).astype(BF16)
        out_ref, h = (low_ref, g) if g < width // 8 else (high_ref, g - width // 8)
        out_ref[h * side : (h + 1) * side, :] = done


def contract(pairs, tiles, green_occ, green_virt):
    width = green_occ.shape[1]
    rows, cols = tiles.shape
    return pl.pallas_call(
        functools.partial(contract_kernel, width, 16),
        in_specs=[IN_SMEM, IN_VMEM, IN_VMEM, IN_VMEM],
        out_specs=[IN_VMEM, IN_VMEM],
        out_shape=[jax.ShapeDtypeStruct((rows // 2, cols), BF16)] * 2,
        scratch_shapes=[pltpu.VMEM((width, width, cols), BF16)],
        compiler_params=pltpu.CompilerParams(vmem_limit_bytes=12 * 2**20),
        cost_estimate=pl.CostEstimate(
            flops=40 * 10**9, bytes_accessed=4 * 2**20, transcendentals=0
        ),
    )(pairs, tiles, green_occ, green_virt)


def products_kernel(pairs, left_at, right_at, turned_at, emit, inputs, scalars, *refs):
    keep_ref, send_ref = refs[inputs : inputs + 2]
    kept = refs[inputs + 2 : -1]
    acc = refs[-1]
    core = scalars[8]

    for h in range(2):
        rights = {q: refs[places[h]][...] for q, places in right_at.items()}
        if emit:
            for n, q in enumerate(right_at):
                kept[2 * n + h][...] = rights[q]
        for p in sorted({p for p, _ in pairs}):
            if p in left_at:
                places = left_at[p]
                rows = rights[pairs[0][1]].shape[0]
                if len(places) == 2:
                    left = refs[places[h]][...].T
                else:
                    left = refs[places[0]][h * rows : (h + 1) * rows, :].T
                if emit:
                    kept[-1][NEAR.index(p), h] = left
            else:
                left = refs[turned_at][NEAR.index(p), h]
            for i, (task_p, q) in enumerate(pairs):
                if task_p == p:
                    part = jnp.dot(left, rights[q], preferred_element_type=F32)
                    acc[i] = part if h == 0 else acc[i] + part
    for i in range(len(pairs)):
        keep_ref[i] = acc[i, pl.ds(pl.multiple_of(core * HALF, HALF), HALF), :]
        other = pl.ds(pl.multiple_of((1 - core) * HALF, HALF), HALF)
        send_ref[i] = acc[i, other, :].astype(BF16)


def products(scalars, lefts, rights, pairs, cost, turned, emit, after):
    operands = []

    def places(blocks):
        operands.extend(blocks)
        return tuple(range(len(operands) - len(blocks), len(operands)))

    raw = sorted({p for p, _ in pairs if turned is None or p not in NEAR})
    left_at = {p: places(lefts[p]) for p in raw}
    right_at = {q: places(rights[q]) for q in sorted({q for _, q in pairs})}
    turned_at = len(operands)
    if turned is not None:
        operands.append(turned)
    specs = [IN_SMEM] + [IN_VMEM] * len(operands)
    for array in after:
        operands.append(array)
        specs.append(pl.BlockSpec(memory_space=pl.ANY))
    count = len(pairs)
    half = rights[pairs[0][1]][0].shape
    shapes = [
        jax.ShapeDtypeStruct((count, HALF, BLOCK), F32),
        jax.ShapeDtypeStruct((count, HALF, BLOCK), BF16),
    ]
    if emit:
        shapes += [jax.ShapeDtypeStruct(half, BF16)] * (2 * len(right_at))
        if turned is None:
            shapes.append(jax.ShapeDtypeStruct((len(NEAR), 2, BLOCK, half[0]), BF16))
    outs = pl.pallas_call(
        functools.partial(
            products_kernel, pairs, left_at, right_at, turned_at, emit, len(operands)
        ),
        in_specs=specs,
        out_specs=[IN_VMEM] * len(shapes),
        out_shape=shapes,
        scratch_shapes=[pltpu.VMEM((count, BLOCK, BLOCK), F32)],
        compiler_params=pltpu.CompilerParams(vmem_limit_bytes=LIMIT * 2**20),
        cost_estimate=pl.CostEstimate(
            flops=cost * 2 * count * 2 * half[0] * BLOCK * BLOCK,
            bytes_accessed=2**20,
            transcendentals=0,
        ),
    )(scalars, *operands)
    kept = {q: tuple(outs[2 + 2 * n : 4 + 2 * n]) for n, q in enumerate(right_at)} if emit else {}
    if emit and turned is None:
        turned = outs[-1]
    return outs[0], outs[1], turned, kept


def merge_kernel(groups, scalars, *refs):
    out_ref = refs[-1]
    for n, pairs in enumerate(groups):
        keep, got = refs[2 * n], refs[2 * n + 1]
        for i, (p, q) in enumerate(pairs):
            target = scalars[SIDE + q] * SIDE + scalars[p]
            out_ref[target] = (keep[i] + got[i].astype(F32)).astype(BF16)


def merge(scalars, groups, halves):
    return pl.pallas_call(
        functools.partial(merge_kernel, groups),
        in_specs=[IN_SMEM] + [IN_VMEM] * len(halves),
        out_specs=IN_VMEM,
        out_shape=jax.ShapeDtypeStruct((SIDE * SIDE, HALF, BLOCK), BF16),
        compiler_params=pltpu.CompilerParams(vmem_limit_bytes=8 * 2**20),
        cost_estimate=pl.CostEstimate(flops=2**20, bytes_accessed=5 * 2**20, transcendentals=0),
    )(scalars, *halves)


def added(core, parts_ref, j):
    total = parts_ref[2 * core + j].astype(F32)
    for y in range(1, SIDE):
        total += parts_ref[y * SIDE + 2 * core + j].astype(F32)
    return -2.0 * total


def theirs_kernel(scalars, parts_ref, out_ref):
    for j in range(2):
        out_ref[j] = added(1 - scalars[8], parts_ref, j)


def theirs(scalars, parts):
    return pl.pallas_call(
        theirs_kernel,
        in_specs=[IN_SMEM, IN_VMEM],
        out_specs=IN_VMEM,
        out_shape=jax.ShapeDtypeStruct((2, HALF, BLOCK), F32),
        compiler_params=pltpu.CompilerParams(vmem_limit_bytes=12 * 2**20),
        cost_estimate=pl.CostEstimate(flops=2**20, bytes_accessed=2 * 2**20, transcendentals=0),
    )(scalars, parts)


def place_kernel(scalars, parts_ref, other_ref, out_ref):
    core = scalars[8]
    own = pl.ds(pl.multiple_of(core * HALF, HALF), HALF)
    rest = pl.ds(pl.multiple_of((1 - core) * HALF, HALF), HALF)
    for j in range(2):
        out_ref[own, j * BLOCK : (j + 1) * BLOCK] = added(core, parts_ref, j)
        out_ref[rest, j * BLOCK : (j + 1) * BLOCK] = other_ref[j]


def place(scalars, parts, other):
    return pl.pallas_call(
        place_kernel,
        in_specs=[IN_SMEM, IN_VMEM, IN_VMEM],
        out_specs=IN_VMEM,
        out_shape=jax.ShapeDtypeStruct((BLOCK, 2 * BLOCK), F32),
        compiler_params=pltpu.CompilerParams(vmem_limit_bytes=12 * 2**20),
        cost_estimate=pl.CostEstimate(flops=2**18, bytes_accessed=2**20, transcendentals=0),
    )(scalars, parts, other)


def ring(block, axis):
    take_next = [((i + 1) % SIDE, i) for i in range(SIDE)]
    take_prev = [((i - 1) % SIDE, i) for i in range(SIDE)]
    return lax.ppermute(block, axis, take_next), lax.ppermute(block, axis, take_prev)


def far(after, before, axis):
    half = after.shape[0] // 2
    take_next = [((i + 1) % SIDE, i) for i in range(SIDE)]
    take_prev = [((i - 1) % SIDE, i) for i in range(SIDE)]
    return (
        lax.ppermute(after[:half], axis, take_next),
        lax.ppermute(before[half:], axis, take_prev),
    )


def around(low, high, axis):
    take_next = [((i + 1) % SIDE, i) for i in range(SIDE)]
    take_prev = [((i - 1) % SIDE, i) for i in range(SIDE)]
    after_low = lax.ppermute(low, axis, take_next)
    before_high = lax.ppermute(high, axis, take_prev)
    after_high = lax.ppermute(high, axis, take_next)
    before_low = lax.ppermute(low, axis, take_prev)
    far_low = lax.ppermute(after_low, axis, take_next)
    far_high = lax.ppermute(before_high, axis, take_prev)
    return {
        0: (low, high),
        1: (after_low, after_high),
        3: (before_low, before_high),
        2: (far_low, far_high),
    }


def per_device(three_centre, tile_list, pair_blocks, green_occ, green_virt):
    y, c, z, x = (lax.axis_index(name) for name in ("y", "c", "z", "x"))
    offsets = jnp.arange(SIDE)
    scalars = jnp.concatenate([(x + offsets) & 3, (z + offsets) & 3, c[None]]).astype(jnp.int32)
    weights = jnp.repeat(tile_list[0].astype(BF16), BLOCK // tile_list.shape[1])
    masked = three_centre * weights[None, :]
    a_after, a_before = ring(masked, "x")
    rights = around(*contract(pair_blocks, masked, green_occ, green_virt), "z")
    lefts = {0: (masked,), 1: (a_after,), 3: (a_before,), 2: far(a_after, a_before, "x")}

    swap = [(0, 1), (1, 0)]
    halves = []
    turned = None
    for pairs, cost in zip(GROUPS, COSTS):
        after = halves[1::2] if pairs == GROUPS[-1] else halves[-2:-1]
        keep, send, turned, kept = products(
            scalars, lefts, rights, pairs, cost, turned, pairs != GROUPS[-1], after
        )
        rights.update(kept)
        halves += [keep, lax.ppermute(send, "c", swap)]
    sends = merge(scalars, GROUPS, halves)
    parts = lax.all_to_all(sends, ("y", "x"), 0, 0)
    return place(scalars, parts, lax.ppermute(theirs(scalars, parts), "c", swap))


def solution(mesh):
    fine = Mesh(mesh.devices.reshape(SIDE, 2, SIDE, SIDE), ("y", "c", "z", "x"))
    ao, aux = ("y", "c"), ("z", "x")
    return jax.shard_map(
        per_device,
        mesh=fine,
        in_specs=(P(ao, aux), P(ao, aux), P(ao, None), P(), P()),
        out_specs=P(aux, ao),
        check_vma=False,
    )
```

```python
import functools

import jax
import jax.numpy as jnp
from jax import lax
from jax.experimental import pallas as pl
from jax.experimental.pallas import tpu as pltpu
from jax.sharding import Mesh, PartitionSpec as P

SIDE = 4
BLOCK = 256
HALF = BLOCK // 2
GROUPS = (
    ((0, 0), (1, 0), (3, 0)),
    ((0, 1), (1, 1), (3, 1), (0, 3), (1, 3), (3, 3)),
    ((2, 0), (2, 1), (2, 3), (0, 2), (1, 2), (3, 2), (2, 2)),
)
COSTS = (10, 1, 1)
NEAR = (0, 1, 3)
LIMIT = 12
LOW = 1920
IN_VMEM = pl.BlockSpec(memory_space=pltpu.VMEM)
IN_SMEM = pl.BlockSpec(memory_space=pltpu.SMEM)
F32 = jnp.float32
BF16 = jnp.bfloat16


def iota(shape, dim):
    return lax.broadcasted_iota(jnp.int32, shape, dim)


def contract_kernel(width, group, pairs, tiles_ref, occ_ref, virt_ref, low_ref, high_ref, half_ref):
    cols = tiles_ref.shape[1]
    tall = width * group
    spread = jnp.where(iota((width, tall), 1) // group == iota((width, tall), 0), 1.0, 0.0)
    wide = jnp.dot(occ_ref[pairs[0, 0]], spread.astype(BF16), preferred_element_type=F32).astype(BF16)
    same = iota((group, tall), 0) == iota((group, tall), 1) % group
    same = jnp.where(same, 1.0, 0.0).astype(BF16)
    occ_wide = (wide[:, None, :] * same[None]).reshape(tall, tall)
    four = 4
    side = four * width
    spread = jnp.where(iota((width, side), 1) % width == iota((width, side), 0), 1.0, 0.0)
    wide = jnp.dot(virt_ref[pairs[0, 1]], spread.astype(BF16), preferred_element_type=F32)
    same = iota((side, side), 0) // width == iota((side, side), 1) // width
    virt_wide = jnp.where(same, jnp.concatenate([wide] * four), 0.0).astype(BF16)

    tiles = tiles_ref.reshape(width, width, cols)
    for t in range(width // group):
        part = tiles[:, t * group : (t + 1) * group, :].reshape(tall, cols)
        half = jnp.dot(occ_wide, part, preferred_element_type=F32).astype(BF16)
        half_ref[:, t * group : (t + 1) * group, :] = half.reshape(width, group, cols)
    for g in range(width // four):
        part = half_ref[g * four : (g + 1) * four].reshape(side, cols)
        done = jnp.dot(virt_wide, part, preferred_element_type=F32).astype(BF16)
        start = g * side
        cut = min(max(LOW - start, 0), side)
        if cut > 0:
            low_ref[start : start + cut, :] = done[:cut]
        if cut < side:
            high_ref[start + cut - LOW : start + side - LOW, :] = done[cut:]


def contract(pairs, tiles, green_occ, green_virt):
    width = green_occ.shape[1]
    rows, cols = tiles.shape
    return pl.pallas_call(
        functools.partial(contract_kernel, width, 16),
        in_specs=[IN_SMEM, IN_VMEM, IN_VMEM, IN_VMEM],
        out_specs=[IN_VMEM, IN_VMEM],
        out_shape=[jax.ShapeDtypeStruct((n, cols), BF16) for n in (LOW, rows - LOW)],
        scratch_shapes=[pltpu.VMEM((width, width, cols), BF16)],
        compiler_params=pltpu.CompilerParams(vmem_limit_bytes=12 * 2**20),
        cost_estimate=pl.CostEstimate(
            flops=40 * 10**9, bytes_accessed=4 * 2**20, transcendentals=0
        ),
    )(pairs, tiles, green_occ, green_virt)


def products_kernel(pairs, left_at, right_at, turned_at, emit, inputs, scalars, *refs):
    keep_ref, send_ref = refs[inputs : inputs + 2]
    kept = refs[inputs + 2 : -1]
    acc = refs[-1]
    core = scalars[8]

    for h in range(2):
        part_of = slice(0, LOW) if h == 0 else slice(LOW, None)
        rights = {q: refs[places[h]][...] for q, places in right_at.items()}
        if emit:
            for n, q in enumerate(right_at):
                kept[2 * n + h][...] = rights[q]
        for p in sorted({p for p, _ in pairs}):
            if p in left_at:
                places = left_at[p]
                if len(places) == 2:
                    left = refs[places[h]][...].T
                else:
                    left = refs[places[0]][part_of, :].T
                if emit:
                    kept[-1][NEAR.index(p), :, part_of] = left
            else:
                left = refs[turned_at][NEAR.index(p), :, part_of]
            for i, (task_p, q) in enumerate(pairs):
                if task_p == p:
                    part = jnp.dot(left, rights[q], preferred_element_type=F32)
                    acc[i] = part if h == 0 else acc[i] + part
    for i in range(len(pairs)):
        keep_ref[i] = acc[i, pl.ds(pl.multiple_of(core * HALF, HALF), HALF), :]
        other = pl.ds(pl.multiple_of((1 - core) * HALF, HALF), HALF)
        send_ref[i] = acc[i, other, :].astype(BF16)


def products(scalars, lefts, rights, pairs, cost, turned, emit, after):
    operands = []

    def places(blocks):
        operands.extend(blocks)
        return tuple(range(len(operands) - len(blocks), len(operands)))

    raw = sorted({p for p, _ in pairs if turned is None or p not in NEAR})
    left_at = {p: places(lefts[p]) for p in raw}
    right_at = {q: places(rights[q]) for q in sorted({q for _, q in pairs})}
    turned_at = len(operands)
    if turned is not None:
        operands.append(turned)
    specs = [IN_SMEM] + [IN_VMEM] * len(operands)
    for array in after:
        operands.append(array)
        specs.append(pl.BlockSpec(memory_space=pl.ANY))
    count = len(pairs)
    rows = sum(half.shape[0] for half in rights[pairs[0][1]])
    shapes = [
        jax.ShapeDtypeStruct((count, HALF, BLOCK), F32),
        jax.ShapeDtypeStruct((count, HALF, BLOCK), BF16),
    ]
    if emit:
        shapes += [jax.ShapeDtypeStruct((n, BLOCK), BF16) for n in (LOW, rows - LOW)] * len(right_at)
        if turned is None:
            shapes.append(jax.ShapeDtypeStruct((len(NEAR), BLOCK, rows), BF16))
    outs = pl.pallas_call(
        functools.partial(
            products_kernel, pairs, left_at, right_at, turned_at, emit, len(operands)
        ),
        in_specs=specs,
        out_specs=[IN_VMEM] * len(shapes),
        out_shape=shapes,
        scratch_shapes=[pltpu.VMEM((count, BLOCK, BLOCK), F32)],
        compiler_params=pltpu.CompilerParams(vmem_limit_bytes=LIMIT * 2**20),
        cost_estimate=pl.CostEstimate(
            flops=cost * 2 * count * rows * BLOCK * BLOCK,
            bytes_accessed=2**20,
            transcendentals=0,
        ),
    )(scalars, *operands)
    kept = {q: tuple(outs[2 + 2 * n : 4 + 2 * n]) for n, q in enumerate(right_at)} if emit else {}
    if emit and turned is None:
        turned = outs[-1]
    return outs[0], outs[1], turned, kept


def merge_kernel(groups, scalars, *refs):
    out_ref = refs[-1]
    for n, pairs in enumerate(groups):
        keep, got = refs[2 * n], refs[2 * n + 1]
        for i, (p, q) in enumerate(pairs):
            target = scalars[SIDE + q] * SIDE + scalars[p]
            out_ref[target] = (keep[i] + got[i].astype(F32)).astype(BF16)


def merge(scalars, groups, halves):
    return pl.pallas_call(
        functools.partial(merge_kernel, groups),
        in_specs=[IN_SMEM] + [IN_VMEM] * len(halves),
        out_specs=IN_VMEM,
        out_shape=jax.ShapeDtypeStruct((SIDE * SIDE, HALF, BLOCK), BF16),
        compiler_params=pltpu.CompilerParams(vmem_limit_bytes=8 * 2**20),
        cost_estimate=pl.CostEstimate(flops=2**20, bytes_accessed=5 * 2**20, transcendentals=0),
    )(scalars, *halves)


def added(core, parts_ref, j):
    total = parts_ref[2 * core + j].astype(F32)
    for y in range(1, SIDE):
        total += parts_ref[y * SIDE + 2 * core + j].astype(F32)
    return -2.0 * total


def theirs_kernel(scalars, parts_ref, out_ref):
    for j in range(2):
        out_ref[j] = added(1 - scalars[8], parts_ref, j)


def theirs(scalars, parts):
    return pl.pallas_call(
        theirs_kernel,
        in_specs=[IN_SMEM, IN_VMEM],
        out_specs=IN_VMEM,
        out_shape=jax.ShapeDtypeStruct((2, HALF, BLOCK), F32),
        compiler_params=pltpu.CompilerParams(vmem_limit_bytes=12 * 2**20),
        cost_estimate=pl.CostEstimate(flops=2**20, bytes_accessed=2 * 2**20, transcendentals=0),
    )(scalars, parts)


def mine_kernel(scalars, parts_ref, out_ref):
    for j in range(2):
        out_ref[:, j * BLOCK : (j + 1) * BLOCK] = added(scalars[8], parts_ref, j)


def mine(scalars, parts):
    return pl.pallas_call(
        mine_kernel,
        grid_spec=pltpu.PrefetchScalarGridSpec(
            num_scalar_prefetch=1,
            grid=(1,),
            in_specs=[IN_VMEM],
            out_specs=pl.BlockSpec((HALF, 2 * BLOCK), lambda i, s: (s[8], 0)),
        ),
        out_shape=jax.ShapeDtypeStruct((BLOCK, 2 * BLOCK), F32),
        compiler_params=pltpu.CompilerParams(vmem_limit_bytes=12 * 2**20),
        cost_estimate=pl.CostEstimate(flops=2**20, bytes_accessed=2**20, transcendentals=0),
    )(scalars, parts)


def place_kernel(scalars, other_ref, whole_ref, out_ref):
    for j in range(2):
        out_ref[:, j * BLOCK : (j + 1) * BLOCK] = other_ref[j]


def place(scalars, other, whole):
    return pl.pallas_call(
        place_kernel,
        grid_spec=pltpu.PrefetchScalarGridSpec(
            num_scalar_prefetch=1,
            grid=(1,),
            in_specs=[IN_VMEM, pl.BlockSpec(memory_space=pl.ANY)],
            out_specs=pl.BlockSpec((HALF, 2 * BLOCK), lambda i, s: (1 - s[8], 0)),
        ),
        out_shape=jax.ShapeDtypeStruct((BLOCK, 2 * BLOCK), F32),
        input_output_aliases={2: 0},
        compiler_params=pltpu.CompilerParams(vmem_limit_bytes=12 * 2**20),
        cost_estimate=pl.CostEstimate(flops=2**18, bytes_accessed=2**19, transcendentals=0),
    )(scalars, other, whole)


def ring(block, axis):
    take_next = [((i + 1) % SIDE, i) for i in range(SIDE)]
    take_prev = [((i - 1) % SIDE, i) for i in range(SIDE)]
    return lax.ppermute(block, axis, take_next), lax.ppermute(block, axis, take_prev)


def far(after, before, axis):
    take_next = [((i + 1) % SIDE, i) for i in range(SIDE)]
    take_prev = [((i - 1) % SIDE, i) for i in range(SIDE)]
    return (
        lax.ppermute(after[:LOW], axis, take_next),
        lax.ppermute(before[LOW:], axis, take_prev),
    )


def around(low, high, axis):
    take_next = [((i + 1) % SIDE, i) for i in range(SIDE)]
    take_prev = [((i - 1) % SIDE, i) for i in range(SIDE)]
    after_low = lax.ppermute(low, axis, take_next)
    before_high = lax.ppermute(high, axis, take_prev)
    after_high = lax.ppermute(high, axis, take_next)
    before_low = lax.ppermute(low, axis, take_prev)
    far_low = lax.ppermute(after_low, axis, take_next)
    far_high = lax.ppermute(before_high, axis, take_prev)
    return {
        0: (low, high),
        1: (after_low, after_high),
        3: (before_low, before_high),
        2: (far_low, far_high),
    }


def per_device(three_centre, tile_list, pair_blocks, green_occ, green_virt):
    y, c, z, x = (lax.axis_index(name) for name in ("y", "c", "z", "x"))
    offsets = jnp.arange(SIDE)
    scalars = jnp.concatenate([(x + offsets) & 3, (z + offsets) & 3, c[None]]).astype(jnp.int32)
    weights = jnp.repeat(tile_list[0].astype(BF16), BLOCK // tile_list.shape[1])
    masked = three_centre * weights[None, :]
    a_after, a_before = ring(masked, "x")
    rights = around(*contract(pair_blocks, masked, green_occ, green_virt), "z")
    lefts = {0: (masked,), 1: (a_after,), 3: (a_before,), 2: far(a_after, a_before, "x")}

    swap = [(0, 1), (1, 0)]
    halves = []
    turned = None
    for pairs, cost in zip(GROUPS, COSTS):
        after = halves[1::2] if pairs == GROUPS[-1] else halves[-2:-1]
        keep, send, turned, kept = products(
            scalars, lefts, rights, pairs, cost, turned, pairs != GROUPS[-1], after
        )
        rights.update(kept)
        halves += [keep, lax.ppermute(send, "c", swap)]
    sends = merge(scalars, GROUPS, halves)
    parts = lax.all_to_all(sends, ("y", "x"), 0, 0)
    other = lax.ppermute(theirs(scalars, parts), "c", swap)
    return place(scalars, other, mine(scalars, parts))


def solution(mesh):
    fine = Mesh(mesh.devices.reshape(SIDE, 2, SIDE, SIDE), ("y", "c", "z", "x"))
    ao, aux = ("y", "c"), ("z", "x")
    return jax.shard_map(
        per_device,
        mesh=fine,
        in_specs=(P(ao, aux), P(ao, aux), P(ao, None), P(), P()),
        out_specs=P(aux, ao),
        check_vma=False,
    )
```

```python
import functools

import jax
import jax.numpy as jnp
from jax import lax
from jax.experimental import pallas as pl
from jax.experimental.pallas import tpu as pltpu
from jax.sharding import Mesh, PartitionSpec as P

SIDE = 4
BLOCK = 256
HALF = BLOCK // 2
GROUPS = (
    ((0, 0), (1, 0), (3, 0)),
    ((0, 1), (1, 1), (3, 1), (0, 3), (1, 3), (3, 3)),
    ((2, 0), (2, 1), (2, 3), (0, 2), (1, 2), (3, 2), (2, 2)),
)
COSTS = (10, 1, 1)
NEAR = (0, 1, 3)
LIMIT = 12
LOW = 1920
IN_VMEM = pl.BlockSpec(memory_space=pltpu.VMEM)
IN_SMEM = pl.BlockSpec(memory_space=pltpu.SMEM)
F32 = jnp.float32
BF16 = jnp.bfloat16


def iota(shape, dim):
    return lax.broadcasted_iota(jnp.int32, shape, dim)


def contract_kernel(width, group, pairs, tiles_ref, occ_ref, virt_ref, low_ref, high_ref, half_ref):
    cols = tiles_ref.shape[1]
    tall = width * group
    spread = jnp.where(iota((width, tall), 1) // group == iota((width, tall), 0), 1.0, 0.0)
    wide = jnp.dot(occ_ref[pairs[0, 0]], spread.astype(BF16), preferred_element_type=F32).astype(BF16)
    same = iota((group, tall), 0) == iota((group, tall), 1) % group
    same = jnp.where(same, 1.0, 0.0).astype(BF16)
    occ_wide = (wide[:, None, :] * same[None]).reshape(tall, tall)
    four = 4
    side = four * width
    spread = jnp.where(iota((width, side), 1) % width == iota((width, side), 0), 1.0, 0.0)
    wide = jnp.dot(virt_ref[pairs[0, 1]], spread.astype(BF16), preferred_element_type=F32)
    same = iota((side, side), 0) // width == iota((side, side), 1) // width
    virt_wide = jnp.where(same, jnp.concatenate([wide] * four), 0.0).astype(BF16)

    tiles = tiles_ref.reshape(width, width, cols)
    for t in range(width // group):
        part = tiles[:, t * group : (t + 1) * group, :].reshape(tall, cols)
        half = jnp.dot(occ_wide, part, preferred_element_type=F32).astype(BF16)
        half_ref[:, t * group : (t + 1) * group, :] = half.reshape(width, group, cols)
    for g in range(width // four):
        part = half_ref[g * four : (g + 1) * four].reshape(side, cols)
        done = jnp.dot(virt_wide, part, preferred_element_type=F32).astype(BF16)
        start = g * side
        cut = min(max(LOW - start, 0), side)
        if cut > 0:
            low_ref[start : start + cut, :] = done[:cut]
        if cut < side:
            high_ref[start + cut - LOW : start + side - LOW, :] = done[cut:]


def contract(pairs, tiles, green_occ, green_virt):
    width = green_occ.shape[1]
    rows, cols = tiles.shape
    return pl.pallas_call(
        functools.partial(contract_kernel, width, 16),
        in_specs=[IN_SMEM, IN_VMEM, IN_VMEM, IN_VMEM],
        out_specs=[IN_VMEM, IN_VMEM],
        out_shape=[jax.ShapeDtypeStruct((n, cols), BF16) for n in (LOW, rows - LOW)],
        scratch_shapes=[pltpu.VMEM((width, width, cols), BF16)],
        compiler_params=pltpu.CompilerParams(vmem_limit_bytes=12 * 2**20),
        cost_estimate=pl.CostEstimate(
            flops=5 * 10**9, bytes_accessed=4 * 2**20, transcendentals=0
        ),
    )(pairs, tiles, green_occ, green_virt)


def products_kernel(pairs, left_at, right_at, turned_at, emit, inputs, scalars, *refs):
    keep_ref, send_ref = refs[inputs : inputs + 2]
    kept = refs[inputs + 2 : -1]
    acc = refs[-1]
    core = scalars[8]

    for h in range(2):
        part_of = slice(0, LOW) if h == 0 else slice(LOW, None)
        rights = {q: refs[places[h]][...] for q, places in right_at.items()}
        if emit:
            for n, q in enumerate(right_at):
                kept[2 * n + h][...] = rights[q]
        for p in sorted({p for p, _ in pairs}):
            if p in left_at:
                places = left_at[p]
                if len(places) == 2:
                    left = refs[places[h]][...].T
                else:
                    left = refs[places[0]][part_of, :].T
                if emit:
                    kept[-1][NEAR.index(p), :, part_of] = left
            else:
                left = refs[turned_at][NEAR.index(p), :, part_of]
            for i, (task_p, q) in enumerate(pairs):
                if task_p == p:
                    part = jnp.dot(left, rights[q], preferred_element_type=F32)
                    acc[i] = part if h == 0 else acc[i] + part
    for i in range(len(pairs)):
        keep_ref[i] = acc[i, pl.ds(pl.multiple_of(core * HALF, HALF), HALF), :]
        other = pl.ds(pl.multiple_of((1 - core) * HALF, HALF), HALF)
        send_ref[i] = acc[i, other, :].astype(BF16)


def products(scalars, lefts, rights, pairs, cost, turned, emit, after):
    operands = []

    def places(blocks):
        operands.extend(blocks)
        return tuple(range(len(operands) - len(blocks), len(operands)))

    raw = sorted({p for p, _ in pairs if turned is None or p not in NEAR})
    left_at = {p: places(lefts[p]) for p in raw}
    right_at = {q: places(rights[q]) for q in sorted({q for _, q in pairs})}
    turned_at = len(operands)
    if turned is not None:
        operands.append(turned)
    specs = [IN_SMEM] + [IN_VMEM] * len(operands)
    for array in after:
        operands.append(array)
        specs.append(pl.BlockSpec(memory_space=pl.ANY))
    count = len(pairs)
    rows = sum(half.shape[0] for half in rights[pairs[0][1]])
    shapes = [
        jax.ShapeDtypeStruct((count, HALF, BLOCK), F32),
        jax.ShapeDtypeStruct((count, HALF, BLOCK), BF16),
    ]
    if emit:
        shapes += [jax.ShapeDtypeStruct((n, BLOCK), BF16) for n in (LOW, rows - LOW)] * len(right_at)
        if turned is None:
            shapes.append(jax.ShapeDtypeStruct((len(NEAR), BLOCK, rows), BF16))
    outs = pl.pallas_call(
        functools.partial(
            products_kernel, pairs, left_at, right_at, turned_at, emit, len(operands)
        ),
        in_specs=specs,
        out_specs=[IN_VMEM] * len(shapes),
        out_shape=shapes,
        scratch_shapes=[pltpu.VMEM((count, BLOCK, BLOCK), F32)],
        compiler_params=pltpu.CompilerParams(vmem_limit_bytes=LIMIT * 2**20),
        cost_estimate=pl.CostEstimate(
            flops=cost * 2 * count * rows * BLOCK * BLOCK,
            bytes_accessed=2**20,
            transcendentals=0,
        ),
    )(scalars, *operands)
    kept = {q: tuple(outs[2 + 2 * n : 4 + 2 * n]) for n, q in enumerate(right_at)} if emit else {}
    if emit and turned is None:
        turned = outs[-1]
    return outs[0], outs[1], turned, kept


def merge_kernel(groups, scalars, *refs):
    out_ref = refs[-1]
    for n, pairs in enumerate(groups):
        keep, got = refs[2 * n], refs[2 * n + 1]
        for i, (p, q) in enumerate(pairs):
            target = scalars[SIDE + q] * SIDE + scalars[p]
            out_ref[target] = (keep[i] + got[i].astype(F32)).astype(BF16)


def merge(scalars, groups, halves):
    return pl.pallas_call(
        functools.partial(merge_kernel, groups),
        in_specs=[IN_SMEM] + [IN_VMEM] * len(halves),
        out_specs=IN_VMEM,
        out_shape=jax.ShapeDtypeStruct((SIDE * SIDE, HALF, BLOCK), BF16),
        compiler_params=pltpu.CompilerParams(vmem_limit_bytes=8 * 2**20),
        cost_estimate=pl.CostEstimate(flops=2**20, bytes_accessed=5 * 2**20, transcendentals=0),
    )(scalars, *halves)


def added(core, parts_ref, j):
    total = parts_ref[2 * core + j].astype(F32)
    for y in range(1, SIDE):
        total += parts_ref[y * SIDE + 2 * core + j].astype(F32)
    return -2.0 * total


def theirs_kernel(scalars, parts_ref, out_ref):
    for j in range(2):
        out_ref[j] = added(1 - scalars[8], parts_ref, j)


def theirs(scalars, parts):
    return pl.pallas_call(
        theirs_kernel,
        in_specs=[IN_SMEM, IN_VMEM],
        out_specs=IN_VMEM,
        out_shape=jax.ShapeDtypeStruct((2, HALF, BLOCK), F32),
        compiler_params=pltpu.CompilerParams(vmem_limit_bytes=12 * 2**20),
        cost_estimate=pl.CostEstimate(flops=2**20, bytes_accessed=2 * 2**20, transcendentals=0),
    )(scalars, parts)


def mine_kernel(scalars, parts_ref, out_ref):
    for j in range(2):
        out_ref[:, j * BLOCK : (j + 1) * BLOCK] = added(scalars[8], parts_ref, j)


def mine(scalars, parts):
    return pl.pallas_call(
        mine_kernel,
        grid_spec=pltpu.PrefetchScalarGridSpec(
            num_scalar_prefetch=1,
            grid=(1,),
            in_specs=[IN_VMEM],
            out_specs=pl.BlockSpec((HALF, 2 * BLOCK), lambda i, s: (s[8], 0)),
        ),
        out_shape=jax.ShapeDtypeStruct((BLOCK, 2 * BLOCK), F32),
        compiler_params=pltpu.CompilerParams(vmem_limit_bytes=12 * 2**20),
        cost_estimate=pl.CostEstimate(flops=2**20, bytes_accessed=2**20, transcendentals=0),
    )(scalars, parts)


def place_kernel(scalars, other_ref, whole_ref, out_ref):
    for j in range(2):
        out_ref[:, j * BLOCK : (j + 1) * BLOCK] = other_ref[j]


def place(scalars, other, whole):
    return pl.pallas_call(
        place_kernel,
        grid_spec=pltpu.PrefetchScalarGridSpec(
            num_scalar_prefetch=1,
            grid=(1,),
            in_specs=[IN_VMEM, pl.BlockSpec(memory_space=pl.ANY)],
            out_specs=pl.BlockSpec((HALF, 2 * BLOCK), lambda i, s: (1 - s[8], 0)),
        ),
        out_shape=jax.ShapeDtypeStruct((BLOCK, 2 * BLOCK), F32),
        input_output_aliases={2: 0},
        compiler_params=pltpu.CompilerParams(vmem_limit_bytes=12 * 2**20),
        cost_estimate=pl.CostEstimate(flops=2**18, bytes_accessed=2**19, transcendentals=0),
    )(scalars, other, whole)


def ring(block, axis):
    take_next = [((i + 1) % SIDE, i) for i in range(SIDE)]
    take_prev = [((i - 1) % SIDE, i) for i in range(SIDE)]
    return lax.ppermute(block, axis, take_next), lax.ppermute(block, axis, take_prev)


def far(after, before, axis):
    take_next = [((i + 1) % SIDE, i) for i in range(SIDE)]
    take_prev = [((i - 1) % SIDE, i) for i in range(SIDE)]
    return (
        lax.ppermute(after[:LOW], axis, take_next),
        lax.ppermute(before[LOW:], axis, take_prev),
    )


def around(low, high, axis):
    take_next = [((i + 1) % SIDE, i) for i in range(SIDE)]
    take_prev = [((i - 1) % SIDE, i) for i in range(SIDE)]
    after_low = lax.ppermute(low, axis, take_next)
    before_high = lax.ppermute(high, axis, take_prev)
    after_high = lax.ppermute(high, axis, take_next)
    before_low = lax.ppermute(low, axis, take_prev)
    far_low = lax.ppermute(after_low, axis, take_next)
    far_high = lax.ppermute(before_high, axis, take_prev)
    return {
        0: (low, high),
        1: (after_low, after_high),
        3: (before_low, before_high),
        2: (far_low, far_high),
    }


def per_device(three_centre, tile_list, pair_blocks, green_occ, green_virt):
    y, c, z, x = (lax.axis_index(name) for name in ("y", "c", "z", "x"))
    offsets = jnp.arange(SIDE)
    scalars = jnp.concatenate([(x + offsets) & 3, (z + offsets) & 3, c[None]]).astype(jnp.int32)
    weights = jnp.repeat(tile_list[0].astype(BF16), BLOCK // tile_list.shape[1])
    masked = three_centre * weights[None, :]
    a_after, a_before = ring(masked, "x")
    rights = around(*contract(pair_blocks, masked, green_occ, green_virt), "z")
    lefts = {0: (masked,), 1: (a_after,), 3: (a_before,), 2: far(a_after, a_before, "x")}

    swap = [(0, 1), (1, 0)]
    halves = []
    turned = None
    for pairs, cost in zip(GROUPS, COSTS):
        after = halves[1::2] if pairs == GROUPS[-1] else halves[-2:-1]
        keep, send, turned, kept = products(
            scalars, lefts, rights, pairs, cost, turned, pairs != GROUPS[-1], after
        )
        rights.update(kept)
        halves += [keep, lax.ppermute(send, "c", swap)]
    sends = merge(scalars, GROUPS, halves)
    parts = lax.all_to_all(sends, ("y", "x"), 0, 0)
    other = lax.ppermute(theirs(scalars, parts), "c", swap)
    return place(scalars, other, mine(scalars, parts))


def solution(mesh):
    fine = Mesh(mesh.devices.reshape(SIDE, 2, SIDE, SIDE), ("y", "c", "z", "x"))
    ao, aux = ("y", "c"), ("z", "x")
    return jax.shard_map(
        per_device,
        mesh=fine,
        in_specs=(P(ao, aux), P(ao, aux), P(ao, None), P(), P()),
        out_specs=P(aux, ao),
        check_vma=False,
    )
```

```python
import functools

import jax
import jax.numpy as jnp
from jax import lax
from jax.experimental import pallas as pl
from jax.experimental.pallas import tpu as pltpu
from jax.sharding import Mesh, PartitionSpec as P

SIDE = 4
BLOCK = 256
HALF = BLOCK // 2
GROUPS = (
    ((0, 0), (1, 0), (3, 0)),
    ((0, 1), (1, 1), (3, 1), (0, 3), (1, 3), (3, 3)),
    ((2, 0), (2, 1), (2, 3), (0, 2), (1, 2), (3, 2), (2, 2)),
)
COSTS = (10, 1, 1)
NEAR = (0, 1, 3)
LIMIT = 24
LOW = 1920
IN_VMEM = pl.BlockSpec(memory_space=pltpu.VMEM)
IN_SMEM = pl.BlockSpec(memory_space=pltpu.SMEM)
F32 = jnp.float32
BF16 = jnp.bfloat16


def iota(shape, dim):
    return lax.broadcasted_iota(jnp.int32, shape, dim)


def contract_kernel(width, group, pairs, tiles_ref, occ_ref, virt_ref, low_ref, high_ref, half_ref):
    cols = tiles_ref.shape[1]
    tall = width * group
    spread = jnp.where(iota((width, tall), 1) // group == iota((width, tall), 0), 1.0, 0.0)
    wide = jnp.dot(occ_ref[pairs[0, 0]], spread.astype(BF16), preferred_element_type=F32).astype(BF16)
    same = iota((group, tall), 0) == iota((group, tall), 1) % group
    same = jnp.where(same, 1.0, 0.0).astype(BF16)
    occ_wide = (wide[:, None, :] * same[None]).reshape(tall, tall)
    four = 4
    side = four * width
    spread = jnp.where(iota((width, side), 1) % width == iota((width, side), 0), 1.0, 0.0)
    wide = jnp.dot(virt_ref[pairs[0, 1]], spread.astype(BF16), preferred_element_type=F32)
    same = iota((side, side), 0) // width == iota((side, side), 1) // width
    virt_wide = jnp.where(same, jnp.concatenate([wide] * four), 0.0).astype(BF16)

    tiles = tiles_ref.reshape(width, width, cols)
    for t in range(width // group):
        part = tiles[:, t * group : (t + 1) * group, :].reshape(tall, cols)
        half = jnp.dot(occ_wide, part, preferred_element_type=F32).astype(BF16)
        half_ref[:, t * group : (t + 1) * group, :] = half.reshape(width, group, cols)
    for g in range(width // four):
        part = half_ref[g * four : (g + 1) * four].reshape(side, cols)
        done = jnp.dot(virt_wide, part, preferred_element_type=F32).astype(BF16)
        start = g * side
        cut = min(max(LOW - start, 0), side)
        if cut > 0:
            low_ref[start : start + cut, :] = done[:cut]
        if cut < side:
            high_ref[start + cut - LOW : start + side - LOW, :] = done[cut:]


def contract(pairs, tiles, green_occ, green_virt):
    width = green_occ.shape[1]
    rows, cols = tiles.shape
    return pl.pallas_call(
        functools.partial(contract_kernel, width, 16),
        in_specs=[IN_SMEM, IN_VMEM, IN_VMEM, IN_VMEM],
        out_specs=[IN_VMEM, IN_VMEM],
        out_shape=[jax.ShapeDtypeStruct((n, cols), BF16) for n in (LOW, rows - LOW)],
        scratch_shapes=[pltpu.VMEM((width, width, cols), BF16)],
        compiler_params=pltpu.CompilerParams(vmem_limit_bytes=12 * 2**20),
        cost_estimate=pl.CostEstimate(
            flops=5 * 10**9, bytes_accessed=4 * 2**20, transcendentals=0
        ),
    )(pairs, tiles, green_occ, green_virt)


def products_kernel(pairs, left_at, right_at, turned_at, emit, inputs, scalars, *refs):
    keep_ref, send_ref = refs[inputs : inputs + 2]
    kept = refs[inputs + 2 : -1]
    acc = refs[-1]
    core = scalars[8]

    for h in range(2):
        part_of = slice(0, LOW) if h == 0 else slice(LOW, None)
        rights = {q: refs[places[h]][...] for q, places in right_at.items()}
        if emit:
            for n, q in enumerate(right_at):
                kept[2 * n + h][...] = rights[q]
        for p in sorted({p for p, _ in pairs}):
            if p in left_at:
                places = left_at[p]
                if len(places) == 2:
                    left = refs[places[h]][...].T
                else:
                    left = refs[places[0]][part_of, :].T
                if emit:
                    kept[-1][NEAR.index(p), :, part_of] = left
            else:
                left = refs[turned_at][NEAR.index(p), :, part_of]
            for i, (task_p, q) in enumerate(pairs):
                if task_p == p:
                    part = jnp.dot(left, rights[q], preferred_element_type=F32)
                    acc[i] = part if h == 0 else acc[i] + part
    for i in range(len(pairs)):
        keep_ref[i] = acc[i, pl.ds(pl.multiple_of(core * HALF, HALF), HALF), :]
        other = pl.ds(pl.multiple_of((1 - core) * HALF, HALF), HALF)
        send_ref[i] = acc[i, other, :].astype(BF16)


def products(scalars, lefts, rights, pairs, cost, turned, emit, after):
    operands = []

    def places(blocks):
        operands.extend(blocks)
        return tuple(range(len(operands) - len(blocks), len(operands)))

    raw = sorted({p for p, _ in pairs if turned is None or p not in NEAR})
    left_at = {p: places(lefts[p]) for p in raw}
    right_at = {q: places(rights[q]) for q in sorted({q for _, q in pairs})}
    turned_at = len(operands)
    if turned is not None:
        operands.append(turned)
    specs = [IN_SMEM] + [IN_VMEM] * len(operands)
    for array in after:
        operands.append(array)
        specs.append(pl.BlockSpec(memory_space=pl.ANY))
    count = len(pairs)
    rows = sum(half.shape[0] for half in rights[pairs[0][1]])
    shapes = [
        jax.ShapeDtypeStruct((count, HALF, BLOCK), F32),
        jax.ShapeDtypeStruct((count, HALF, BLOCK), BF16),
    ]
    if emit:
        shapes += [jax.ShapeDtypeStruct((n, BLOCK), BF16) for n in (LOW, rows - LOW)] * len(right_at)
        if turned is None:
            shapes.append(jax.ShapeDtypeStruct((len(NEAR), BLOCK, rows), BF16))
    outs = pl.pallas_call(
        functools.partial(
            products_kernel, pairs, left_at, right_at, turned_at, emit, len(operands)
        ),
        in_specs=specs,
        out_specs=[IN_VMEM] * len(shapes),
        out_shape=shapes,
        scratch_shapes=[pltpu.VMEM((count, BLOCK, BLOCK), F32)],
        compiler_params=pltpu.CompilerParams(vmem_limit_bytes=LIMIT * 2**20),
        cost_estimate=pl.CostEstimate(
            flops=cost * 2 * count * rows * BLOCK * BLOCK,
            bytes_accessed=2**20,
            transcendentals=0,
        ),
    )(scalars, *operands)
    kept = {q: tuple(outs[2 + 2 * n : 4 + 2 * n]) for n, q in enumerate(right_at)} if emit else {}
    if emit and turned is None:
        turned = outs[-1]
    return outs[0], outs[1], turned, kept


def merge_kernel(groups, scalars, *refs):
    out_ref = refs[-1]
    for n, pairs in enumerate(groups):
        keep, got = refs[2 * n], refs[2 * n + 1]
        for i, (p, q) in enumerate(pairs):
            target = scalars[SIDE + q] * SIDE + scalars[p]
            out_ref[target] = (keep[i] + got[i].astype(F32)).astype(BF16)


def merge(scalars, groups, halves):
    return pl.pallas_call(
        functools.partial(merge_kernel, groups),
        in_specs=[IN_SMEM] + [IN_VMEM] * len(halves),
        out_specs=IN_VMEM,
        out_shape=jax.ShapeDtypeStruct((SIDE * SIDE, HALF, BLOCK), BF16),
        compiler_params=pltpu.CompilerParams(vmem_limit_bytes=8 * 2**20),
        cost_estimate=pl.CostEstimate(flops=2**20, bytes_accessed=5 * 2**20, transcendentals=0),
    )(scalars, *halves)


def added(core, parts_ref, j):
    total = parts_ref[2 * core + j].astype(F32)
    for y in range(1, SIDE):
        total += parts_ref[y * SIDE + 2 * core + j].astype(F32)
    return -2.0 * total


def theirs_kernel(scalars, parts_ref, out_ref):
    for j in range(2):
        out_ref[j] = added(1 - scalars[8], parts_ref, j)


def theirs(scalars, parts):
    return pl.pallas_call(
        theirs_kernel,
        in_specs=[IN_SMEM, IN_VMEM],
        out_specs=IN_VMEM,
        out_shape=jax.ShapeDtypeStruct((2, HALF, BLOCK), F32),
        compiler_params=pltpu.CompilerParams(vmem_limit_bytes=12 * 2**20),
        cost_estimate=pl.CostEstimate(flops=2**20, bytes_accessed=2 * 2**20, transcendentals=0),
    )(scalars, parts)


def mine_kernel(scalars, parts_ref, out_ref):
    for j in range(2):
        out_ref[:, j * BLOCK : (j + 1) * BLOCK] = added(scalars[8], parts_ref, j)


def mine(scalars, parts):
    return pl.pallas_call(
        mine_kernel,
        grid_spec=pltpu.PrefetchScalarGridSpec(
            num_scalar_prefetch=1,
            grid=(1,),
            in_specs=[IN_VMEM],
            out_specs=pl.BlockSpec((HALF, 2 * BLOCK), lambda i, s: (s[8], 0)),
        ),
        out_shape=jax.ShapeDtypeStruct((BLOCK, 2 * BLOCK), F32),
        compiler_params=pltpu.CompilerParams(vmem_limit_bytes=12 * 2**20),
        cost_estimate=pl.CostEstimate(flops=2**20, bytes_accessed=2**20, transcendentals=0),
    )(scalars, parts)


def place_kernel(scalars, other_ref, whole_ref, out_ref):
    for j in range(2):
        out_ref[:, j * BLOCK : (j + 1) * BLOCK] = other_ref[j]


def place(scalars, other, whole):
    return pl.pallas_call(
        place_kernel,
        grid_spec=pltpu.PrefetchScalarGridSpec(
            num_scalar_prefetch=1,
            grid=(1,),
            in_specs=[IN_VMEM, pl.BlockSpec(memory_space=pl.ANY)],
            out_specs=pl.BlockSpec((HALF, 2 * BLOCK), lambda i, s: (1 - s[8], 0)),
        ),
        out_shape=jax.ShapeDtypeStruct((BLOCK, 2 * BLOCK), F32),
        input_output_aliases={2: 0},
        compiler_params=pltpu.CompilerParams(vmem_limit_bytes=12 * 2**20),
        cost_estimate=pl.CostEstimate(flops=2**18, bytes_accessed=2**19, transcendentals=0),
    )(scalars, other, whole)


def ring(block, axis):
    take_next = [((i + 1) % SIDE, i) for i in range(SIDE)]
    take_prev = [((i - 1) % SIDE, i) for i in range(SIDE)]
    return lax.ppermute(block, axis, take_next), lax.ppermute(block, axis, take_prev)


def far(after, before, axis):
    take_next = [((i + 1) % SIDE, i) for i in range(SIDE)]
    take_prev = [((i - 1) % SIDE, i) for i in range(SIDE)]
    return (
        lax.ppermute(after[:LOW], axis, take_next),
        lax.ppermute(before[LOW:], axis, take_prev),
    )


def around(low, high, axis):
    take_next = [((i + 1) % SIDE, i) for i in range(SIDE)]
    take_prev = [((i - 1) % SIDE, i) for i in range(SIDE)]
    after_low = lax.ppermute(low, axis, take_next)
    before_high = lax.ppermute(high, axis, take_prev)
    after_high = lax.ppermute(high, axis, take_next)
    before_low = lax.ppermute(low, axis, take_prev)
    far_low = lax.ppermute(after_low, axis, take_next)
    far_high = lax.ppermute(before_high, axis, take_prev)
    return {
        0: (low, high),
        1: (after_low, after_high),
        3: (before_low, before_high),
        2: (far_low, far_high),
    }


def per_device(three_centre, tile_list, pair_blocks, green_occ, green_virt):
    y, c, z, x = (lax.axis_index(name) for name in ("y", "c", "z", "x"))
    offsets = jnp.arange(SIDE)
    scalars = jnp.concatenate([(x + offsets) & 3, (z + offsets) & 3, c[None]]).astype(jnp.int32)
    weights = jnp.repeat(tile_list[0].astype(BF16), BLOCK // tile_list.shape[1])
    masked = three_centre * weights[None, :]
    a_after, a_before = ring(masked, "x")
    rights = around(*contract(pair_blocks, masked, green_occ, green_virt), "z")
    lefts = {0: (masked,), 1: (a_after,), 3: (a_before,), 2: far(a_after, a_before, "x")}

    swap = [(0, 1), (1, 0)]
    halves = []
    turned = None
    for pairs, cost in zip(GROUPS, COSTS):
        after = halves[1::2] if pairs == GROUPS[-1] else halves[-2:-1]
        keep, send, turned, kept = products(
            scalars, lefts, rights, pairs, cost, turned, pairs != GROUPS[-1], after
        )
        rights.update(kept)
        halves += [keep, lax.ppermute(send, "c", swap)]
    sends = merge(scalars, GROUPS, halves)
    parts = lax.all_to_all(sends, ("y", "x"), 0, 0)
    other = lax.ppermute(theirs(scalars, parts), "c", swap)
    return place(scalars, other, mine(scalars, parts))


def solution(mesh):
    fine = Mesh(mesh.devices.reshape(SIDE, 2, SIDE, SIDE), ("y", "c", "z", "x"))
    ao, aux = ("y", "c"), ("z", "x")
    return jax.shard_map(
        per_device,
        mesh=fine,
        in_specs=(P(ao, aux), P(ao, aux), P(ao, None), P(), P()),
        out_specs=P(aux, ao),
        check_vma=False,
    )
```
